128 devices in a mesh: shard: 16 (over y, x), sub: 8 (over z, core).
Axes of the slice: x: 4, y: 4, z: 4, core: 2. Of those that a mesh axis runs over, the one named last changes fastest.
Arguments:
- queries: bfloat16 [256, 2048], P(('shard', 'sub')), may hold values from -128 to 128
- passages: bfloat16 [262144, 2048], P(('shard', 'sub')), may hold values from -32 to 32
- candidates: int32 [256, 200], P(('shard', 'sub')), may hold values from 0 to 262143, as said below
Outputs:
- coarse_lse: float32 [256], P(('shard', 'sub'))
- cand_probs: float32 [256, 200], P(('shard', 'sub'))
- pooled: bfloat16 [256, 2048], P(('shard', 'sub'))
The draws below stay inside these ranges and needn't reach their ends.
Inputs may be any that keep to these rules, and one draw needn't show every extreme that they name: Every id names a passage. Among the 200 candidates of the 2 queries owned by one device (aligned blocks of rows), at most 8 name passages held by one device (id // 2048); in every block at least two owners are named exactly 8 times, one of them the same owner for every block.
All inputs are finite; a program needn't handle non-finite values.
Results may differ from the reference program's by a relative error of at most 0.0025.
The reference program's roundings to bfloat16 on the way (of `cand_rows` and `cand_weights`) count: a program that leaves them out, or rounds other values in their place, can miss the bound.
Values may be sent and summed in bfloat16 or wider, within the bound.
A program may use at most 64 MiB of HBM per device.

```python
import jax
import jax.numpy as jnp
from jax import lax

D = 2048
PREFIX = 64
CANDS = 200
PAS_DEV = 2048
QRY_DEV = 2
PASSAGES = 262144
QUERIES = 256
CAP = 8


def row_values(key, row_ids):
    base = jax.random.fold_in(key, 101)
    return jax.vmap(lambda index: jnp.clip(jax.random.normal(jax.random.fold_in(base, index), (D,), jnp.float32), -4.0, 4.0))(row_ids)


def prefix_factor(key, row_ids, rise):
    owners_all = PASSAGES // PAS_DEV
    order = jax.random.permutation(jax.random.fold_in(key, 404), owners_all).astype(jnp.int32)
    owner = row_ids // PAS_DEV
    ranked = jnp.take(order, owner).astype(jnp.float32)
    factor = 1.0 + rise * ranked / (owners_all - 1)
    columns = jnp.arange(D, dtype=jnp.int32) < PREFIX
    return jnp.where(columns[None, :], factor[:, None], 1.0)


def candidate_ids(key):
    blocks = QUERIES // QRY_DEV
    needed = QRY_DEV * CANDS
    base = jax.random.fold_in(key, 303)
    shuffled = jax.random.permutation(jax.random.fold_in(base, 0), blocks)
    global_hot = shuffled[0]
    popular = shuffled[1:5]
    entries = jnp.arange(blocks * CAP, dtype=jnp.int32) // CAP

    def one_block(block):
        ranks = jax.random.permutation(jax.random.fold_in(base, 1000 + block), blocks * CAP).astype(jnp.int32)
        block_hot = popular[block % 4]
        priority = jnp.where(entries == global_hot, -2, jnp.where(entries == block_hot, -1, ranks))
        chosen = jnp.argsort(priority, stable=True)[:needed]
        owners = entries[chosen]
        owners = owners[jax.random.permutation(jax.random.fold_in(base, 2000 + block), needed)]
        local_ids = jax.random.randint(jax.random.fold_in(base, 3000 + block), (needed,), 0, PAS_DEV, jnp.int32)
        return owners * PAS_DEV + local_ids
    all_ids = jax.vmap(one_block)(jnp.arange(blocks, dtype=jnp.int32))
    return all_ids.reshape(QUERIES, CANDS).astype(jnp.int32)


def draw_candidates(key, part):
    return candidate_ids(key)


def draw_passages(key, part):
    row_ids = jnp.arange(PASSAGES, dtype=jnp.int32)
    values = row_values(key, row_ids)
    values = values * prefix_factor(key, row_ids, 2.0)
    return values.astype(jnp.bfloat16)


def draw_queries(key, part):
    values = jnp.clip(jax.random.normal(jax.random.fold_in(key, 7), (QUERIES, D), jnp.float32), -4.0, 4.0)
    return values.astype(jnp.bfloat16)


def setup_inputs(seed: int = 0) -> dict:
    key_of = jax.random.split(jax.random.key(seed), 4)
    return {
        "queries": draw_queries(jax.random.fold_in(key_of[3], 71), 0),
        "passages": draw_passages(jax.random.fold_in(key_of[3], 71), 0),
        "candidates": draw_candidates(jax.random.fold_in(key_of[3], 71), 0),
    }


def reference(queries, passages, candidates):
    prefix_queries = queries[:, :PREFIX]
    prefix_blocks = passages[:, :PREFIX].reshape(PASSAGES // PAS_DEV, PAS_DEV, PREFIX)

    def scan_block(carry, block_rows):
        highest, total = carry
        scores = jnp.dot(prefix_queries, block_rows.T, preferred_element_type=jnp.float32) * (PREFIX ** -0.5)
        new_high = jnp.maximum(highest, jnp.max(scores, axis=1))
        total = total * jnp.exp(highest - new_high) + jnp.sum(jnp.exp(scores - new_high[:, None]), axis=1)
        return (new_high, total), None

    start_high = jnp.full((QUERIES,), -jnp.inf, jnp.float32)
    start_total = jnp.zeros((QUERIES,), jnp.float32)
    (highest, total), unused = lax.scan(scan_block, (start_high, start_total), prefix_blocks)
    coarse_lse = highest + jnp.log(total)

    group = 16 if QUERIES % 16 == 0 else 1
    query_groups = queries.reshape(QUERIES // group, group, D)
    cand_groups = candidates.reshape(QUERIES // group, group, CANDS)

    def rescore(inputs):
        query_rows, cand_ids = inputs
        cand_rows = jnp.take(passages, cand_ids.reshape(-1), axis=0).reshape(group, CANDS, D)
        scores = jnp.einsum("qd,qcd->qc", query_rows.astype(jnp.float32), cand_rows.astype(jnp.float32)) * (D ** -0.5)
        cand_probs = jax.nn.softmax(scores, axis=1)
        cand_weights = cand_probs.astype(jnp.bfloat16)
        pooled = jnp.einsum("qc,qcd->qd", cand_weights.astype(jnp.float32), cand_rows.astype(jnp.float32))
        return cand_probs, pooled.astype(jnp.bfloat16)

    cand_probs, pooled = lax.map(rescore, (query_groups, cand_groups))
    return coarse_lse, cand_probs.reshape(QUERIES, CANDS), pooled.reshape(QUERIES, D)
```

```python
import jax
import jax.numpy as jnp
from jax import lax
from jax.experimental import pallas as pl
from jax.experimental.pallas import tpu as pltpu
from jax.sharding import PartitionSpec as P

NSH, NSU = 16, 8
NDEV = NSH * NSU
D = 2048
HALF = D // 2
PREFIX = 64
CANDS = 200
CAP = 8
NQ = 256
CHUNKS = 4
CW = D // CHUNKS
NEG = -3.0e38
MESH = pl.DeviceIdType.MESH
F32, BF16, I32 = jnp.float32, jnp.bfloat16, jnp.int32


def iota(shape, dim):
    return lax.broadcasted_iota(I32, shape, dim)


def dot_nt(a, b):
    return lax.dot_general(a, b, (((1,), (1,)), ((), ())), preferred_element_type=F32)


def kernel(cand_ref, q_ref, p_hbm, lse_ref, probs_ref, out_ref,
           p_v, candp, qf, qsend, code, qbuf, cbuf, q16f, q16, qall, ctile, crecv,
           st, stat1, stat1r, stat2, stat2r, codet, wt, whi, wlo,
           pool, ra, rb, zsend, zr, psend, prtile, pusend, purecv,
           p_sem, q1s, q1r, c1s, c1r, q2s, q2r, c2s, c2r, sibs, sibr,
           s1s, s1r, s2s, s2r, ps_s, ps_r, pu_s, pu_r, as_, ar_, bs_, br_, zs_, zr_):
    sh, su = lax.axis_index("shard"), lax.axis_index("sub")
    core, z = su % 2, su // 2

    def sub_peer(k):
        return (sh, su ^ k)

    def shard_peer(k):
        return (sh ^ k, su)

    barrier = pltpu.get_barrier_semaphore()

    def greet(k, c):
        pl.semaphore_signal(barrier, inc=1, device_id=shard_peer(k), device_id_type=MESH)
        return c

    def greet_sub(k, c):
        pl.semaphore_signal(barrier, inc=1, device_id=sub_peer(k), device_id_type=MESH)
        return c

    lax.fori_loop(1, NSH, greet, 0)
    lax.fori_loop(1, NSU, greet_sub, 0)
    load_p = pltpu.make_async_copy(p_hbm, p_v, p_sem)
    load_p.start()

    def loop(n, fn):
        def step(k, c):
            fn(k)
            return c
        lax.fori_loop(1, n, step, 0)

    def remote(src, dst, s, r, peer):
        return pltpu.make_async_remote_copy(src_ref=src, dst_ref=dst, send_sem=s, recv_sem=r,
                                            device_id=peer, device_id_type=MESH)

    candp[...] = jnp.full((2, 256), -1, I32)
    candp[:, :CANDS] = cand_ref[...]
    upper = jnp.where(iota((256, 256), 0) <= iota((256, 256), 1), 1.0, 0.0).astype(BF16)
    onehots, ranks = [], []
    before = jnp.zeros((128, 1), F32)
    for t in range(2):
        ids = candp[t:t + 1, :]
        dev = ids // D
        place = jnp.where(ids >= 0, (dev % NSU) * NSH + dev // NSU, -1)
        local = ids - dev * D + 1
        oh = jnp.where(iota((128, 256), 0) == place, 1.0, 0.0)
        ohb = oh.astype(BF16)
        cum = jnp.dot(ohb, upper, preferred_element_type=F32) + before
        rank = jnp.sum(oh * cum, axis=0, keepdims=True) - 1.0
        before = cum[:, 255:256]
        at = iota((CAP, 256), 0).astype(F32) == rank
        high = jnp.where(at, (local // 64).astype(F32), 0.0)
        low = jnp.where(at, (local % 64).astype(F32), 0.0)
        parts = dot_nt(jnp.concatenate([high, low], axis=0).astype(BF16), ohb)
        code[t * 8:t * 8 + 8, :] = parts[:8] * 64.0 + parts[8:]
        onehots.append(ohb)
        ranks.append(rank)

    x = q_ref[...].astype(F32)
    for r in range(8):
        qf[2 * r:2 * r + 2, :] = x[:, r * 256:(r + 1) * 256]
    qsend[...] = qf[...].astype(BF16)
    qbuf[su] = qsend[...]
    cbuf[su] = code[...]

    pl.semaphore_wait(barrier, NSH - 1 + NSU - 1)

    def d_q1(k):
        return remote(qsend, qbuf.at[su], q1s.at[k], q1r.at[k], sub_peer(k))

    def d_c1(k):
        return remote(code, cbuf.at[su], c1s.at[k], c1r.at[k], sub_peer(k))

    def start1(k):
        d_q1(k).start()
        d_c1(k).start()

    def wait1(k):
        d_q1(k).wait()
        d_c1(k).wait()

    loop(NSU, start1)
    loop(NSU, wait1)

    for i in range(NSU):
        block = qbuf[i].astype(F32)
        for r in range(8):
            for t in range(2):
                row = (i % 2) * 8 + t * 4 + i // 2
                q16f[row:row + 1, r * 256:(r + 1) * 256] = block[2 * r + t:2 * r + t + 1, :]
    for h in range(2):
        q16[h] = q16f[:, h * HALF:(h + 1) * HALF].astype(BF16)
    lane = iota((8, 128), 1)
    base = (sh % 8) * 16
    tiles = [jnp.zeros((8, 128), F32) for _ in range(NSH)]
    for i in range(NSU):
        for t in range(2):
            mine = pltpu.roll(cbuf[i, t * 8:t * 8 + 8, :], (NSU - su) * NSH, 1)
            here = lane == base + ((i % 2) * 8 + t * 4 + i // 2)
            for j in range(NSH):
                tiles[j] = jnp.where(here, jnp.broadcast_to(mine[:, j:j + 1], (8, 128)), tiles[j])
    for j in range(NSH):
        ctile[j] = tiles[j]
    qall[core, pl.ds(pl.multiple_of(sh * 16, 16), 16), :] = q16[core]
    crecv[sh] = ctile[sh]

    def d_q2(k):
        rows = pl.ds(pl.multiple_of(sh * 16, 16), 16)
        return remote(q16.at[core], qall.at[core, rows], q2s.at[k], q2r.at[k], shard_peer(k))

    def d_c2(k):
        return remote(ctile.at[sh ^ k], crecv.at[sh], c2s.at[k], c2r.at[k], shard_peer(k))

    def start2(k):
        d_q2(k).start()
        d_c2(k).start()

    def wait2(k):
        d_q2(k).wait()
        d_c2(k).wait()

    loop(NSH, start2)
    loop(NSH, wait2)
    sib = remote(qall.at[core], qall.at[core], sibs, sibr, sub_peer(1))
    sib.start()

    load_p.wait()
    ROWS = 256

    def score_half(h, add):
        def step(i, c):
            rows = pl.ds(pl.multiple_of(i * ROWS, ROWS), ROWS)
            cols = pl.ds(pl.multiple_of(h * HALF, HALF), HALF)
            part = dot_nt(p_v[rows, cols], qall[h])
            st[rows, :] = st[rows, :] + part if add else part
            return c
        lax.fori_loop(0, D // ROWS, step, 0)

    score_half(core, False)
    sib.wait()
    score_half(1 - core, True)

    first, second = crecv[0], crecv[8]
    for i in range(1, 8):
        first = first + crecv[i]
        second = second + crecv[8 + i]
    codes = jnp.concatenate([first, second], axis=1).astype(I32) - 1
    rows_of = [jnp.broadcast_to(codes[s:s + 1, :], (8, 256)) for s in range(CAP)]
    sub_iota = iota((8, 256), 0)

    def pick(i, accs):
        for j in range(4):
            start = pl.multiple_of(i * 32 + j * 8, 8)
            vals = st[pl.ds(start, 8), :]
            at = sub_iota + start
            accs = tuple(a + jnp.where(at == rows_of[s], vals, 0.0) for s, a in enumerate(accs))
        return accs

    accs = lax.fori_loop(0, D // 32, pick, tuple(jnp.zeros((8, 256), F32) for _ in range(CAP)))
    scores = jnp.concatenate([jnp.sum(a, axis=0, keepdims=True) for a in accs], axis=0) * (D ** -0.5)
    valid = codes >= 0
    masked = jnp.where(valid, scores, NEG)
    m0 = jnp.max(masked, axis=0, keepdims=True)
    l0 = jnp.sum(jnp.where(valid, jnp.exp(masked - m0), 0.0), axis=0, keepdims=True)
    stat1[0:1, :] = m0
    stat1[1:2, :] = l0
    stat1[2:8, :] = jnp.zeros((6, 256), F32)
    stat1r[su] = stat1[...]

    def d_s1(k):
        return remote(stat1, stat1r.at[su], s1s.at[k], s1r.at[k], sub_peer(k))

    loop(NSU, lambda k: d_s1(k).start())

    qp = qall[0, :, 0:128]
    qp = jnp.where(iota((NQ, 128), 1) < PREFIX, qp.astype(F32), 0.0).astype(BF16)

    def prefix(i, top):
        rows = pl.ds(pl.multiple_of(i * ROWS, ROWS), ROWS)
        part = dot_nt(p_v[rows, 0:128], qp) * (PREFIX ** -0.5)
        st[rows, :] = part
        return jnp.maximum(top, jnp.max(part.reshape(ROWS // 8, 8, 256), axis=0))

    top = lax.fori_loop(0, D // ROWS, prefix, jnp.full((8, 256), NEG, F32))
    cm = jnp.max(top, axis=0, keepdims=True)

    def expsum(i, tot):
        rows = pl.ds(pl.multiple_of(i * 64, 64), 64)
        return tot + jnp.sum(jnp.exp(st[rows, :] - cm).reshape(8, 8, 256), axis=0)

    tot = lax.fori_loop(0, D // 64, expsum, jnp.zeros((8, 256), F32))
    cl = jnp.sum(tot, axis=0, keepdims=True)

    loop(NSU, lambda k: d_s1(k).wait())

    def join(buf, n, row):
        top = buf[0, row:row + 1, :]
        for i in range(1, n):
            top = jnp.maximum(top, buf[i, row:row + 1, :])
        total = jnp.zeros((1, 256), F32)
        for i in range(n):
            total = total + buf[i, row + 1:row + 2, :] * jnp.exp(buf[i, row:row + 1, :] - top)
        return top, total

    m1, l1 = join(stat1r, NSU, 0)
    stat2[0:1, :] = m1
    stat2[1:2, :] = l1
    stat2[2:3, :] = cm
    stat2[3:4, :] = cl
    stat2[4:8, :] = jnp.zeros((4, 256), F32)
    stat2r[sh] = stat2[...]

    def d_s2(k):
        return remote(stat2, stat2r.at[sh], s2s.at[k], s2r.at[k], shard_peer(k))

    loop(NSH, lambda k: d_s2(k).start())
    codet[:, 0:8] = codes.astype(F32).T
    loop(NSH, lambda k: d_s2(k).wait())
    m2, l2 = join(stat2r, NSH, 0)
    cm2, cl2 = join(stat2r, NSH, 2)

    probs = jnp.where(valid, jnp.exp(masked - m2), 0.0) / l2
    weights = probs.astype(BF16).astype(F32)
    wt[:, 0:8] = weights.T
    psend[0] = probs[:, 0:128]
    psend[1] = probs[:, 128:256]

    def spread(i, c):
        rows = pl.ds(pl.multiple_of(i * 16, 16), 16)
        ct = codet[rows, 0:8].astype(I32)
        w = wt[rows, 0:8]
        for g in range(4):
            cols = iota((16, 512), 1) + g * 512
            val = jnp.zeros((16, 512), F32)
            for s in range(CAP):
                val = val + jnp.where(cols == ct[:, s:s + 1], w[:, s:s + 1], 0.0)
            hi = val.astype(BF16)
            whi[rows, g * 512:(g + 1) * 512] = hi
            wlo[rows, g * 512:(g + 1) * 512] = (val - hi.astype(F32)).astype(BF16)
        return c

    lax.fori_loop(0, NQ // 16, spread, 0)

    def d_a(j):
        return remote(pool.at[j, 1 - core], ra.at[j], as_.at[j], ar_.at[j], sub_peer(1))

    def d_b(j, k):
        return remote(pool.at[j, core, sh ^ k], rb.at[j, sh], bs_.at[j, k], br_.at[j, k], shard_peer(k))

    def multiply(j):
        cols = slice(j * CW, (j + 1) * CW)
        part = jnp.dot(whi[...], p_v[:, cols], preferred_element_type=F32)
        part = part + jnp.dot(wlo[...], p_v[:, cols], preferred_element_type=F32)
        for i in range(NSH):
            for c in range(2):
                pool[j, c, i] = part[i * 16 + c * 8:i * 16 + c * 8 + 8, :]
        d_a(j).start()

    def forward(j):
        d_a(j).wait()
        for i in range(NSH):
            pool[j, core, i] = pool[j, core, i] + ra[j, i]
        rb[j, sh] = pool[j, core, sh]
        loop(NSH, lambda k: d_b(j, k).start())

    def d_ps(k):
        return remote(psend.at[(sh ^ k) // 8], prtile.at[sh], ps_s.at[k], ps_r.at[k], shard_peer(k))

    multiply(0)
    for j in range(1, CHUNKS):
        multiply(j)
        forward(j - 1)
    forward(CHUNKS - 1)

    prtile[sh] = psend[sh // 8]
    loop(NSH, lambda k: d_ps(k).start())
    loop(NSH, lambda k: d_ps(k).wait())
    outs = [[jnp.zeros((8, 128), F32) for _ in range(2)] for _ in range(NSU)]
    for h in range(NSH):
        mine = pltpu.roll(prtile[h], 128 - base, 1)
        here = lane == su * NSH + h
        for d in range(NSU):
            for t in range(2):
                col = (d % 2) * 8 + t * 4 + d // 2
                outs[d][t] = jnp.where(here, jnp.broadcast_to(mine[:, col:col + 1], (8, 128)), outs[d][t])
    coarse = jnp.concatenate([cm2[:, 0:128], cm2[:, 128:256], cl2[:, 0:128], cl2[:, 128:256],
                              jnp.zeros((4, 128), F32)], axis=0)
    for d in range(NSU):
        for t in range(2):
            pusend[d, t * 8:t * 8 + 8, :] = outs[d][t]
        pusend[d, 16:24, :] = coarse
    purecv[su] = pusend[su]

    def d_pu(k):
        return remote(pusend.at[su ^ k], purecv.at[su], pu_s.at[k], pu_r.at[k], sub_peer(k))

    loop(NSU, lambda k: d_pu(k).start())

    for j in range(CHUNKS):
        loop(NSH, lambda k: d_b(j, k).wait())
        tile = rb[j, 0]
        for i in range(1, NSH):
            tile = tile + rb[j, i]
        for t in range(2):
            for i in range(4):
                zsend[i, t * 4 + j:t * 4 + j + 1, :] = tile[t * 4 + i:t * 4 + i + 1, :]
    zr[z] = zsend[z]

    def d_z(k):
        return remote(zsend.at[z ^ k], zr.at[z], zs_.at[k], zr_.at[k], sub_peer(2 * k))

    loop(4, lambda k: d_z(k).start())

    loop(NSU, lambda k: d_pu(k).wait())
    for t in range(2):
        p = purecv[0, t * 8:t * 8 + 8, :]
        for i in range(1, NSU):
            p = p + purecv[i, t * 8:t * 8 + 8, :]
        p1 = p.astype(BF16)
        rest = p - p1.astype(F32)
        p2 = rest.astype(BF16)
        p3 = (rest - p2.astype(F32)).astype(BF16)
        y = jnp.dot(jnp.concatenate([p1.astype(F32), p2.astype(F32), p3.astype(F32)], axis=0).astype(BF16),
                    onehots[t], preferred_element_type=F32)
        y = y[0:8] + y[8:16] + y[16:24]
        row = jnp.sum(jnp.where(iota((CAP, 256), 0).astype(F32) == ranks[t], y, 0.0), axis=0, keepdims=True)
        probs_ref[t:t + 1, :] = row[:, :CANDS]
    top = purecv[0, 16:18, :]
    for i in range(1, NSU):
        top = jnp.maximum(top, purecv[i, 16:18, :])
    total = jnp.zeros((2, 128), F32)
    for i in range(NSU):
        total = total + purecv[i, 18:20, :] * jnp.exp(purecv[i, 16:18, :] - top)
    lse = top + jnp.log(total)
    spot = iota((2, 128), 0) * 128 + iota((2, 128), 1)
    for t in range(2):
        mine = jnp.where(spot == sh * 16 + core * 8 + t * 4 + z, lse, 0.0)
        lse_ref[0:1, t:t + 1] = jnp.sum(mine, keepdims=True)

    loop(4, lambda k: d_z(k).wait())
    final = zr[0] + zr[1] + zr[2] + zr[3]
    for t in range(2):
        for j in range(CHUNKS):
            out_ref[t:t + 1, j * CW:(j + 1) * CW] = final[t * 4 + j:t * 4 + j + 1, :].astype(BF16)


def shards(queries, passages, candidates):
    vmem = pl.BlockSpec(memory_space=pltpu.VMEM)
    V, DMA = pltpu.VMEM, pltpu.SemaphoreType.DMA
    lse, probs, pooled = pl.pallas_call(
        kernel,
        name="retrieve",
        out_shape=(
            jax.ShapeDtypeStruct((1, 2), F32),
            jax.ShapeDtypeStruct((2, CANDS), F32),
            jax.ShapeDtypeStruct((2, D), BF16),
        ),
        in_specs=[vmem, vmem, pl.BlockSpec(memory_space=pl.ANY)],
        out_specs=(vmem, vmem, vmem),
        scratch_shapes=[
            V((D, D), BF16), V((2, 256), I32), V((16, 256), F32), V((16, 256), BF16), V((16, 128), F32),
            V((NSU, 16, 256), BF16), V((NSU, 16, 128), F32), V((16, D), F32), V((2, 16, HALF), BF16),
            V((2, NQ, HALF), BF16), V((NSH, 8, 128), F32), V((NSH, 8, 128), F32),
            V((D, NQ), F32),
            V((8, 256), F32), V((NSU, 8, 256), F32), V((8, 256), F32), V((NSH, 8, 256), F32),
            V((NQ, 128), F32), V((NQ, 128), F32), V((NQ, D), BF16), V((NQ, D), BF16),
            V((CHUNKS, 2, NSH, 8, CW), F32), V((CHUNKS, NSH, 8, CW), F32), V((CHUNKS, NSH, 8, CW), F32),
            V((4, 8, CW), F32), V((4, 8, CW), F32), V((2, 8, 128), F32), V((NSH, 8, 128), F32),
            V((NSU, 24, 128), F32), V((NSU, 24, 128), F32),
            DMA(()),
            DMA((NSU,)), DMA((NSU,)), DMA((NSU,)), DMA((NSU,)),
            DMA((NSH,)), DMA((NSH,)), DMA((NSH,)), DMA((NSH,)), DMA(()), DMA(()),
            DMA((NSU,)), DMA((NSU,)), DMA((NSH,)), DMA((NSH,)),
            DMA((NSH,)), DMA((NSH,)), DMA((NSU,)), DMA((NSU,)),
            DMA((CHUNKS,)), DMA((CHUNKS,)), DMA((CHUNKS, NSH)), DMA((CHUNKS, NSH)),
            DMA((4,)), DMA((4,)),
        ],
        compiler_params=pltpu.CompilerParams(
            collective_id=0, has_side_effects=True, vmem_limit_bytes=50 * 1024 * 1024
        ),
    )(candidates, queries, passages)
    return lse.reshape(2), probs, pooled


def solution(mesh):
    spec = P(("shard", "sub"), None)
    return jax.shard_map(shards, mesh=mesh, in_specs=(spec, spec, spec),
                         out_specs=(P(("shard", "sub")), spec, spec), check_vma=False)
```

```python
import jax
import jax.numpy as jnp
from jax import lax
from jax.experimental import pallas as pl
from jax.experimental.pallas import tpu as pltpu
from jax.sharding import PartitionSpec as P

NSH, NSU = 16, 8
NDEV = NSH * NSU
D = 2048
HALF = D // 2
PREFIX = 64
CANDS = 200
CAP = 8
NQ = 256
CHUNKS = 4
CW = D // CHUNKS
NEG = -3.0e38
MESH = pl.DeviceIdType.MESH
F32, BF16, I32 = jnp.float32, jnp.bfloat16, jnp.int32


def iota(shape, dim):
    return lax.broadcasted_iota(I32, shape, dim)


def dot_nt(a, b):
    return lax.dot_general(a, b, (((1,), (1,)), ((), ())), preferred_element_type=F32)


def kernel(cand_hbm, q_hbm, p_hbm, lse_ref, probs_ref, out_ref,
           p_v, cand_v, q_v, candp, qf, qsend, code, qbuf, cbuf, q16f, q16, qall, ctile, crecv,
           st, cst, stat1, stat1r, stat2, stat2r, colt, count, grown, whl,
           pool, ra, rb, re, zsend, zr, psend, prtile, pusend, purecv,
           p_sem, in_sem, q1s, q1r, c1s, c1r, q2s, q2r, q3s, q3r, c2s, c2r, sibs, sibr,
           s1s, s1r, s2s, s2r, ps_s, ps_r, pu_s, pu_r, as_, ar_, bs_, br_, es_, er_, zs_, zr_):
    sh, su = lax.axis_index("shard"), lax.axis_index("sub")
    core, z = su % 2, su // 2
    y, x = sh // 4, sh % 4
    a1, a2 = y + core * (x - y), x + core * (y - x)
    step1, step2 = 4 - 3 * core, 1 + 3 * core

    def sub_peer(k):
        return (sh, su ^ k)

    def shard_peer(k):
        return (sh ^ k, su)

    load_c = pltpu.make_async_copy(cand_hbm, cand_v, in_sem.at[0])
    load_c.start()
    load_q = pltpu.make_async_copy(q_hbm, q_v, in_sem.at[1])
    load_q.start()
    barrier = pltpu.get_barrier_semaphore()

    def greet(k, c):
        pl.semaphore_signal(barrier, inc=1, device_id=shard_peer(k), device_id_type=MESH)
        return c

    def greet_sub(k, c):
        pl.semaphore_signal(barrier, inc=1, device_id=sub_peer(k), device_id_type=MESH)
        return c

    lax.fori_loop(1, NSH, greet, 0)
    lax.fori_loop(1, NSU, greet_sub, 0)
    load_p = pltpu.make_async_copy(p_hbm, p_v, p_sem)
    load_p.start()

    def loop(n, fn):
        def step(k, c):
            fn(k)
            return c
        lax.fori_loop(1, n, step, 0)

    def remote(src, dst, s, r, peer):
        return pltpu.make_async_remote_copy(src_ref=src, dst_ref=dst, send_sem=s, recv_sem=r,
                                            device_id=peer, device_id_type=MESH)

    candp[...] = jnp.full((2, 256), -1, I32)
    load_c.wait()
    candp[:, :CANDS] = cand_v[...]
    upper = jnp.where(iota((256, 256), 0) <= iota((256, 256), 1), 1.0, 0.0).astype(BF16)
    onehots, ranks = [], []
    before = jnp.zeros((128, 1), F32)
    for t in range(2):
        ids = candp[t:t + 1, :]
        dev = ids // D
        place = jnp.where(ids >= 0, (dev % NSU) * NSH + dev // NSU, -1)
        local = ids - dev * D + 1
        oh = jnp.where(iota((128, 256), 0) == place, 1.0, 0.0)
        ohb = oh.astype(BF16)
        cum = jnp.dot(ohb, upper, preferred_element_type=F32) + before
        rank = jnp.sum(oh * cum, axis=0, keepdims=True) - 1.0
        before = cum[:, 255:256]
        at = iota((CAP, 256), 0).astype(F32) == rank
        high = jnp.where(at, (local // 64).astype(F32), 0.0)
        low = jnp.where(at, (local % 64).astype(F32), 0.0)
        parts = dot_nt(jnp.concatenate([high, low], axis=0).astype(BF16), ohb)
        code[t * 8:t * 8 + 8, :] = parts[:8] * 64.0 + parts[8:]
        onehots.append(ohb)
        ranks.append(rank)

    load_q.wait()
    qs = q_v[...].astype(F32)
    for r in range(8):
        qf[2 * r:2 * r + 2, :] = qs[:, r * 256:(r + 1) * 256]
    qsend[...] = qf[...].astype(BF16)
    qbuf[su] = qsend[...]
    cbuf[su] = code[...]

    pl.semaphore_wait(barrier, NSH - 1 + NSU - 1)

    def d_q1(k):
        return remote(qsend, qbuf.at[su], q1s.at[k], q1r.at[k], sub_peer(k))

    def d_c1(k):
        return remote(code, cbuf.at[su], c1s.at[k], c1r.at[k], sub_peer(k))

    def start1(k):
        d_q1(k).start()
        d_c1(k).start()

    def wait1(k):
        d_q1(k).wait()
        d_c1(k).wait()

    loop(NSU, start1)
    loop(NSU, wait1)

    for i in range(NSU):
        block = qbuf[i].astype(F32)
        for r in range(8):
            for t in range(2):
                row = (i % 2) * 8 + t * 4 + i // 2
                q16f[row:row + 1, r * 256:(r + 1) * 256] = block[2 * r + t:2 * r + t + 1, :]
    for h in range(2):
        q16[h] = q16f[:, h * HALF:(h + 1) * HALF].astype(BF16)
    lane = iota((8, 128), 1)
    base = (sh % 8) * 16
    tiles = [jnp.zeros((8, 128), F32) for _ in range(NSH)]
    for i in range(NSU):
        for t in range(2):
            mine = pltpu.roll(cbuf[i, t * 8:t * 8 + 8, :], (NSU - su) * NSH, 1)
            here = lane == base + ((i % 2) * 8 + t * 4 + i // 2)
            for j in range(NSH):
                tiles[j] = jnp.where(here, jnp.broadcast_to(mine[:, j:j + 1], (8, 128)), tiles[j])
    for j in range(NSH):
        ctile[j] = tiles[j]
    qall[core, pl.ds(pl.multiple_of(sh * 16, 16), 16), :] = q16[core]
    crecv[sh] = ctile[sh]

    def q_block(j):
        return qall.at[core, pl.ds(pl.multiple_of((sh ^ (j * step1)) * 16, 16), 16)]

    def d_q2(k):
        return remote(q_block(0), q_block(0), q2s.at[k], q2r.at[k], shard_peer(k * step1))

    def d_q3(j, k):
        return remote(q_block(j), q_block(j), q3s.at[j, k], q3r.at[j, k], shard_peer(k * step2))

    def d_c2(k):
        return remote(ctile.at[sh ^ k], crecv.at[sh], c2s.at[k], c2r.at[k], shard_peer(k))

    loop(4, lambda k: d_q2(k).start())
    loop(4, lambda k: d_q3(0, k).start())
    loop(NSH, lambda k: d_c2(k).start())
    for j in range(1, 4):
        d_q2(j).wait()
        loop(4, lambda k: d_q3(j, k).start())
    for j in range(4):
        loop(4, lambda k: d_q3(j, k).wait())
    loop(NSH, lambda k: d_c2(k).wait())
    sib = remote(qall.at[core], qall.at[core], sibs, sibr, sub_peer(1))
    sib.start()

    load_p.wait()
    ROWS = 512

    def score_half(h, add):
        def step(i, c):
            rows = pl.ds(pl.multiple_of(i * ROWS, ROWS), ROWS)
            cols = pl.ds(pl.multiple_of(h * HALF, HALF), HALF)
            part = dot_nt(p_v[rows, cols], qall[h])
            st[rows, :] = st[rows, :] + part if add else part
            return c
        lax.fori_loop(0, D // ROWS, step, 0)

    score_half(core, False)
    sib.wait()
    score_half(1 - core, True)

    first, second = crecv[0], crecv[8]
    for i in range(1, 8):
        first = first + crecv[i]
        second = second + crecv[8 + i]
    codes = jnp.concatenate([first, second], axis=1).astype(I32) - 1
    rows_of = [jnp.broadcast_to(codes[s:s + 1, :], (8, 256)) for s in range(CAP)]
    sub_iota = iota((8, 256), 0)

    def pick(i, accs):
        for j in range(4):
            start = pl.multiple_of(i * 32 + j * 8, 8)
            vals = st[pl.ds(start, 8), :]
            at = sub_iota + start
            accs = tuple(a + jnp.where(at == rows_of[s], vals, 0.0) for s, a in enumerate(accs))
        return accs

    accs = lax.fori_loop(0, D // 32, pick, tuple(jnp.zeros((8, 256), F32) for _ in range(CAP)))
    scores = jnp.concatenate([jnp.sum(a, axis=0, keepdims=True) for a in accs], axis=0) * (D ** -0.5)
    valid = codes >= 0
    masked = jnp.where(valid, scores, NEG)
    m0 = jnp.max(masked, axis=0, keepdims=True)
    l0 = jnp.sum(jnp.where(valid, jnp.exp(masked - m0), 0.0), axis=0, keepdims=True)
    stat1[0:1, :] = m0
    stat1[1:2, :] = l0
    stat1[2:8, :] = jnp.zeros((6, 256), F32)
    stat1r[su] = stat1[...]

    def d_s1(k):
        return remote(stat1, stat1r.at[su], s1s.at[k], s1r.at[k], sub_peer(k))

    loop(NSU, lambda k: d_s1(k).start())

    qp = qall[0, :, 0:128]
    qp = jnp.where(iota((NQ, 128), 1) < PREFIX, qp.astype(F32), 0.0).astype(BF16)

    def prefix(i, top):
        rows = pl.ds(pl.multiple_of(i * ROWS, ROWS), ROWS)
        part = dot_nt(p_v[rows, 0:128], qp) * (PREFIX ** -0.5)
        cst[rows, :] = part
        return jnp.maximum(top, jnp.max(part.reshape(ROWS // 8, 8, 256), axis=0))

    top = lax.fori_loop(0, D // ROWS, prefix, jnp.full((8, 256), NEG, F32))
    cm = jnp.max(top, axis=0, keepdims=True)

    def expsum(i, tot):
        rows = pl.ds(pl.multiple_of(i * 64, 64), 64)
        return tot + jnp.sum(jnp.exp(cst[rows, :] - cm).reshape(8, 8, 256), axis=0)

    tot = lax.fori_loop(0, D // 64, expsum, jnp.zeros((8, 256), F32))
    cl = jnp.sum(tot, axis=0, keepdims=True)

    loop(NSU, lambda k: d_s1(k).wait())

    def join(buf, n, row):
        top = buf[0, row:row + 1, :]
        for i in range(1, n):
            top = jnp.maximum(top, buf[i, row:row + 1, :])
        total = jnp.zeros((1, 256), F32)
        for i in range(n):
            total = total + buf[i, row + 1:row + 2, :] * jnp.exp(buf[i, row:row + 1, :] - top)
        return top, total

    m1, l1 = join(stat1r, NSU, 0)
    stat2[0:1, :] = m1
    stat2[1:2, :] = l1
    stat2[2:3, :] = cm
    stat2[3:4, :] = cl
    stat2[4:8, :] = jnp.zeros((4, 256), F32)
    stat2r[sh] = stat2[...]

    def d_s2(k):
        return remote(stat2, stat2r.at[sh], s2s.at[k], s2r.at[k], shard_peer(k))

    loop(NSH, lambda k: d_s2(k).start())

    colt[:, 0:8] = codes.astype(F32).T
    colt[:, 8:16] = jnp.broadcast_to(m0, (8, 256)).T

    def flip(i, c):
        rows = pl.ds(pl.multiple_of(i * 256, 256), 256)
        grown[:, rows] = st[rows, :].T
        return c

    lax.fori_loop(0, D // 256, flip, 0)

    def tally(i, c):
        rows = pl.ds(pl.multiple_of(i * 16, 16), 16)
        ct = colt[rows, 0:8].astype(I32)
        top = colt[rows, 8:9]
        for g in range(4):
            cols = iota((16, 512), 1) + g * 512
            here = slice(g * 512, (g + 1) * 512)
            val = jnp.zeros((16, 512), F32)
            for s in range(CAP):
                val = val + jnp.where(cols == ct[:, s:s + 1], 1.0, 0.0)
            count[rows, here] = val
            grown[rows, here] = jnp.where(val > 0.0, jnp.exp(grown[rows, here] * (D ** -0.5) - top), 0.0)
        return c

    lax.fori_loop(0, NQ // 16, tally, 0)
    loop(NSH, lambda k: d_s2(k).wait())
    m2, l2 = join(stat2r, NSH, 0)
    cm2, cl2 = join(stat2r, NSH, 2)

    scale = jnp.exp(m0 - m2) / l2
    probs = jnp.where(valid, jnp.exp(masked - m0), 0.0) * scale
    psend[0] = probs[:, 0:128]
    psend[1] = probs[:, 128:256]
    prtile[sh] = psend[sh // 8]

    def d_ps(k):
        return remote(psend.at[(sh ^ k) // 8], prtile.at[sh], ps_s.at[k], ps_r.at[k], shard_peer(k))

    loop(NSH, lambda k: d_ps(k).start())

    colt[:, 16:24] = jnp.broadcast_to(scale, (8, 256)).T

    def spread(i, c):
        rows = pl.ds(pl.multiple_of(i * 16, 16), 16)
        lows = pl.ds(pl.multiple_of(NQ + i * 16, 16), 16)
        f = colt[rows, 16:17]
        val = (grown[rows, :] * f).astype(BF16).astype(F32) * count[rows, :]
        hi = val.astype(BF16)
        whl[rows, :] = hi
        whl[lows, :] = (val - hi.astype(F32)).astype(BF16)
        return c

    lax.fori_loop(0, NQ // 16, spread, 0)

    def d_a(j):
        return remote(pool.at[j, 1 - core], ra.at[j], as_.at[j], ar_.at[j], sub_peer(1))

    def d_b(j, k):
        return remote(pool.at[j, core, pl.ds((a1 ^ k) * 4, 4)], rb.at[j, pl.ds(k * 4, 4)],
                      bs_.at[j, k], br_.at[j, k], shard_peer(k * step1))

    def d_e(j, k):
        return remote(rb.at[j, a2 ^ k], re.at[j, k], es_.at[j, k], er_.at[j, k], shard_peer(k * step2))

    def multiply(j):
        cols = slice(j * CW, (j + 1) * CW)
        part = jnp.dot(whl[...], p_v[:, cols], preferred_element_type=F32)
        part = part[:NQ] + part[NQ:]
        for i in range(NSH):
            for c in range(2):
                pool[j, c, i if c == 0 else (i % 4) * 4 + i // 4] = part[i * 16 + c * 8:i * 16 + c * 8 + 8, :]
        d_a(j).start()

    def forward(j):
        d_a(j).wait()
        for i in range(NSH):
            pool[j, core, i] = pool[j, core, i] + ra[j, i]
        loop(4, lambda k: d_b(j, k).start())

    def second(j):
        loop(4, lambda k: d_b(j, k).wait())
        for i in range(4):
            rb[j, i] = pool[j, core, a1 * 4 + i] + rb[j, 4 + i] + rb[j, 8 + i] + rb[j, 12 + i]
        loop(4, lambda k: d_e(j, k).start())

    def third(j):
        loop(4, lambda k: d_e(j, k).wait())
        tile = rb[j, a2] + re[j, 1] + re[j, 2] + re[j, 3]
        for t in range(2):
            for i in range(4):
                zsend[i, t * 4 + j:t * 4 + j + 1, :] = tile[t * 4 + i:t * 4 + i + 1, :]

    multiply(0)
    multiply(1)
    forward(0)
    multiply(2)
    forward(1)
    multiply(3)
    forward(2)
    second(0)
    forward(3)

    loop(NSH, lambda k: d_ps(k).wait())
    outs = [[jnp.zeros((8, 128), F32) for _ in range(2)] for _ in range(NSU)]
    for h in range(NSH):
        mine = pltpu.roll(prtile[h], 128 - base, 1)
        here = lane == su * NSH + h
        for d in range(NSU):
            for t in range(2):
                col = (d % 2) * 8 + t * 4 + d // 2
                outs[d][t] = jnp.where(here, jnp.broadcast_to(mine[:, col:col + 1], (8, 128)), outs[d][t])
    coarse = jnp.concatenate([cm2[:, 0:128], cm2[:, 128:256], cl2[:, 0:128], cl2[:, 128:256],
                              jnp.zeros((4, 128), F32)], axis=0)
    for d in range(NSU):
        for t in range(2):
            pusend[d, t * 8:t * 8 + 8, :] = outs[d][t]
        pusend[d, 16:24, :] = coarse
    purecv[su] = pusend[su]

    def d_pu(k):
        return remote(pusend.at[su ^ k], purecv.at[su], pu_s.at[k], pu_r.at[k], sub_peer(k))

    loop(NSU, lambda k: d_pu(k).start())

    second(1)
    third(0)
    second(2)
    third(1)
    second(3)
    third(2)
    third(3)
    zr[z] = zsend[z]

    def d_z(k):
        return remote(zsend.at[z ^ k], zr.at[z], zs_.at[k], zr_.at[k], sub_peer(2 * k))

    loop(4, lambda k: d_z(k).start())

    loop(NSU, lambda k: d_pu(k).wait())
    for t in range(2):
        p = purecv[0, t * 8:t * 8 + 8, :]
        for i in range(1, NSU):
            p = p + purecv[i, t * 8:t * 8 + 8, :]
        p1 = p.astype(BF16)
        rest = p - p1.astype(F32)
        p2 = rest.astype(BF16)
        p3 = (rest - p2.astype(F32)).astype(BF16)
        y = jnp.dot(jnp.concatenate([p1.astype(F32), p2.astype(F32), p3.astype(F32)], axis=0).astype(BF16),
                    onehots[t], preferred_element_type=F32)
        y = y[0:8] + y[8:16] + y[16:24]
        row = jnp.sum(jnp.where(iota((CAP, 256), 0).astype(F32) == ranks[t], y, 0.0), axis=0, keepdims=True)
        probs_ref[t:t + 1, :] = row[:, :CANDS]
    top = purecv[0, 16:18, :]
    for i in range(1, NSU):
        top = jnp.maximum(top, purecv[i, 16:18, :])
    total = jnp.zeros((2, 128), F32)
    for i in range(NSU):
        total = total + purecv[i, 18:20, :] * jnp.exp(purecv[i, 16:18, :] - top)
    lse = top + jnp.log(total)
    spot = iota((2, 128), 0) * 128 + iota((2, 128), 1)
    for t in range(2):
        mine = jnp.where(spot == sh * 16 + core * 8 + t * 4 + z, lse, 0.0)
        lse_ref[0:1, t:t + 1] = jnp.sum(mine, keepdims=True)

    loop(4, lambda k: d_z(k).wait())
    final = zr[0] + zr[1] + zr[2] + zr[3]
    for t in range(2):
        for j in range(CHUNKS):
            out_ref[t:t + 1, j * CW:(j + 1) * CW] = final[t * 4 + j:t * 4 + j + 1, :].astype(BF16)


def shards(queries, passages, candidates):
    vmem = pl.BlockSpec(memory_space=pltpu.VMEM)
    V, DMA = pltpu.VMEM, pltpu.SemaphoreType.DMA
    lse, probs, pooled = pl.pallas_call(
        kernel,
        name="retrieve",
        out_shape=(
            jax.ShapeDtypeStruct((1, 2), F32),
            jax.ShapeDtypeStruct((2, CANDS), F32),
            jax.ShapeDtypeStruct((2, D), BF16),
        ),
        in_specs=[pl.BlockSpec(memory_space=pl.ANY)] * 3,
        out_specs=(vmem, vmem, vmem),
        scratch_shapes=[
            V((D, D), BF16), V((2, CANDS), I32), V((2, D), BF16), V((2, 256), I32), V((16, 256), F32), V((16, 256), BF16), V((16, 128), F32),
            V((NSU, 16, 256), BF16), V((NSU, 16, 128), F32), V((16, D), F32), V((2, 16, HALF), BF16),
            V((2, NQ, HALF), BF16), V((NSH, 8, 128), F32), V((NSH, 8, 128), F32),
            V((D, NQ), F32), V((D, NQ), F32),
            V((8, 256), F32), V((NSU, 8, 256), F32), V((8, 256), F32), V((NSH, 8, 256), F32),
            V((NQ, 128), F32), V((NQ, D), F32), V((NQ, D), F32), V((2 * NQ, D), BF16),
            V((CHUNKS, 2, NSH, 8, CW), F32), V((CHUNKS, NSH, 8, CW), F32), V((CHUNKS, NSH, 8, CW), F32),
            V((CHUNKS, 4, 8, CW), F32),
            V((4, 8, CW), F32), V((4, 8, CW), F32), V((2, 8, 128), F32), V((NSH, 8, 128), F32),
            V((NSU, 24, 128), F32), V((NSU, 24, 128), F32),
            DMA(()), DMA((2,)),
            DMA((NSU,)), DMA((NSU,)), DMA((NSU,)), DMA((NSU,)),
            DMA((4,)), DMA((4,)), DMA((4, 4)), DMA((4, 4)), DMA((NSH,)), DMA((NSH,)), DMA(()), DMA(()),
            DMA((NSU,)), DMA((NSU,)), DMA((NSH,)), DMA((NSH,)),
            DMA((NSH,)), DMA((NSH,)), DMA((NSU,)), DMA((NSU,)),
            DMA((CHUNKS,)), DMA((CHUNKS,)), DMA((CHUNKS, 4)), DMA((CHUNKS, 4)), DMA((CHUNKS, 4)), DMA((CHUNKS, 4)),
            DMA((4,)), DMA((4,)),
        ],
        compiler_params=pltpu.CompilerParams(
            collective_id=0, has_side_effects=True, vmem_limit_bytes=50 * 1024 * 1024
        ),
    )(candidates, queries, passages)
    return lse.reshape(2), probs, pooled


def solution(mesh):
    spec = P(("shard", "sub"), None)
    return jax.shard_map(shards, mesh=mesh, in_specs=(spec, spec, spec),
                         out_specs=(P(("shard", "sub")), spec, spec), check_vma=False)
```

```python
import jax
import jax.numpy as jnp
from jax import lax
from jax.experimental import pallas as pl
from jax.experimental.pallas import tpu as pltpu
from jax.sharding import PartitionSpec as P

NSH, NSU = 16, 8
NDEV = NSH * NSU
D = 2048
QW = D // 4
LAST = 256
PREFIX = 64
CANDS = 200
CAP = 8
NQ = 256
CHUNKS = 4
CW = D // CHUNKS
TWO_HOP = CHUNKS - 1
NEG = -3.0e38
MESH = pl.DeviceIdType.MESH
F32, BF16, I32 = jnp.float32, jnp.bfloat16, jnp.int32


def iota(shape, dim):
    return lax.broadcasted_iota(I32, shape, dim)


def dot_nt(a, b):
    return lax.dot_general(a, b, (((1,), (1,)), ((), ())), preferred_element_type=F32)


def kernel(cand_hbm, q_hbm, p_hbm, lse_ref, probs_ref, out_ref,
           p_v, cand_v, q_v, candp, qf, qsend, code, qbuf, cbuf, q16f, q16, qall, ctile, crecv,
           st, cst, stat1, stat1r, stat2, stat2r, colt, count, grown, whl,
           pool, ra, rb, re, zsend, zr, lsend, lrecv, psend, prtile, pusend, purecv,
           p_sem, in_sem, q1s, q1r, c1s, c1r, q2s, q2r, q3s, q3r, c2s, c2r, sibs, sibr,
           s1s, s1r, s2s, s2r, ps_s, ps_r, pu_s, pu_r, as_, ar_, bs_, br_, es_, er_, zs_, zr_, ls_, lr_):
    sh, su = lax.axis_index("shard"), lax.axis_index("sub")
    core, z = su % 2, su // 2
    y, x = sh // 4, sh % 4
    a1, a2 = y + core * (x - y), x + core * (y - x)
    step1, step2 = 4 - 3 * core, 1 + 3 * core

    def sub_peer(k):
        return (sh, su ^ k)

    def shard_peer(k):
        return (sh ^ k, su)

    barrier = pltpu.get_barrier_semaphore()

    def greet(k, c):
        pl.semaphore_signal(barrier, inc=1, device_id=shard_peer(k), device_id_type=MESH)
        return c

    def greet_sub(k, c):
        pl.semaphore_signal(barrier, inc=1, device_id=sub_peer(k), device_id_type=MESH)
        return c

    lax.fori_loop(1, NSH, greet, 0)
    lax.fori_loop(1, NSU, greet_sub, 0)
    load_p = pltpu.make_async_copy(p_hbm, p_v, p_sem)
    load_p.start()

    def loop(n, fn):
        for k in range(1, n):
            fn(k)

    def remote(src, dst, s, r, peer):
        return pltpu.make_async_remote_copy(src_ref=src, dst_ref=dst, send_sem=s, recv_sem=r,
                                            device_id=peer, device_id_type=MESH)

    qs = q_hbm[...].astype(F32)
    for r in range(8):
        qf[2 * r:2 * r + 2, :] = qs[:, r * 256:(r + 1) * 256]
    qsend[...] = qf[...].astype(BF16)
    qbuf[su] = qsend[...]

    pl.semaphore_wait(barrier, NSH - 1 + NSU - 1)

    def d_q1(k):
        return remote(qsend, qbuf.at[su], q1s.at[k], q1r.at[k], sub_peer(k))

    def d_c1(k):
        return remote(code, cbuf.at[su], c1s.at[k], c1r.at[k], sub_peer(k))

    loop(NSU, lambda k: d_q1(k).start())

    candp[...] = jnp.full((2, 256), -1, I32)
    candp[:, :CANDS] = cand_hbm[...]
    upper = jnp.where(iota((256, 256), 0) <= iota((256, 256), 1), 1.0, 0.0).astype(BF16)
    onehots, ranks = [], []
    before = jnp.zeros((128, 1), F32)
    for t in range(2):
        ids = candp[t:t + 1, :]
        dev = ids // D
        place = jnp.where(ids >= 0, (dev % NSU) * NSH + dev // NSU, -1)
        local = ids - dev * D + 1
        oh = jnp.where(iota((128, 256), 0) == place, 1.0, 0.0)
        ohb = oh.astype(BF16)
        cum = jnp.dot(ohb, upper, preferred_element_type=F32) + before
        rank = jnp.sum(oh * cum, axis=0, keepdims=True) - 1.0
        before = cum[:, 255:256]
        at = iota((CAP, 256), 0).astype(F32) == rank
        high = jnp.where(at, (local // 64).astype(F32), 0.0)
        low = jnp.where(at, (local % 64).astype(F32), 0.0)
        parts = dot_nt(jnp.concatenate([high, low], axis=0).astype(BF16), ohb)
        code[t * 8:t * 8 + 8, :] = parts[:8] * 64.0 + parts[8:]
        onehots.append(ohb)
        ranks.append(rank)

    cbuf[su] = code[...]
    loop(NSU, lambda k: d_c1(k).start())
    loop(NSU, lambda k: d_q1(k).wait())
    for i in range(NSU):
        block = qbuf[i].astype(F32)
        for r in range(8):
            for t in range(2):
                row = (i % 2) * 8 + t * 4 + i // 2
                q16f[row:row + 1, r * 256:(r + 1) * 256] = block[2 * r + t:2 * r + t + 1, :]
    for h in range(4):
        q16[h] = q16f[:, h * QW:(h + 1) * QW].astype(BF16)
    for c in range(2):
        qall[core * 2 + c, pl.ds(pl.multiple_of(sh * 16, 16), 16), :] = q16[core * 2 + c]

    def q_block(j):
        return qall.at[pl.ds(core * 2, 2), pl.ds(pl.multiple_of((sh ^ (j * step1)) * 16, 16), 16)]

    def d_q2(k):
        return remote(q_block(0), q_block(0), q2s.at[k], q2r.at[k], shard_peer(k * step1))

    def d_q3(j, k):
        return remote(q_block(j), q_block(j), q3s.at[j, k], q3r.at[j, k], shard_peer(k * step2))

    def d_c2(k):
        return remote(ctile.at[sh ^ k], crecv.at[sh], c2s.at[k], c2r.at[k], shard_peer(k))

    loop(4, lambda k: d_q2(k).start())
    loop(4, lambda k: d_q3(0, k).start())
    for j in range(1, 4):
        d_q2(j).wait()
        loop(4, lambda k: d_q3(j, k).start())

    loop(NSU, lambda k: d_c1(k).wait())
    lane = iota((8, 128), 1)
    base = (sh % 8) * 16
    tiles = [jnp.zeros((8, 128), F32) for _ in range(NSH)]
    for i in range(NSU):
        for t in range(2):
            mine = pltpu.roll(cbuf[i, t * 8:t * 8 + 8, :], (NSU - su) * NSH, 1)
            here = lane == base + ((i % 2) * 8 + t * 4 + i // 2)
            for j in range(NSH):
                tiles[j] = jnp.where(here, jnp.broadcast_to(mine[:, j:j + 1], (8, 128)), tiles[j])
    for j in range(NSH):
        ctile[j] = tiles[j]
    crecv[sh] = ctile[sh]
    loop(NSH, lambda k: d_c2(k).start())
    for j in range(4):
        loop(4, lambda k: d_q3(j, k).wait())
    def d_sib(c):
        part = qall.at[core * 2 + c]
        return remote(part, part, sibs.at[c], sibr.at[c], sub_peer(1))

    d_sib(0).start()
    d_sib(1).start()
    load_p.wait()

    def score(h, rows):
        cols = pl.ds(pl.multiple_of(h * QW, QW), QW)
        return dot_nt(p_v[rows, cols], qall[h])

    def score_half(i, c):
        rows = pl.ds(pl.multiple_of(i * 512, 512), 512)
        st[rows, :] = score(core * 2, rows) + score(core * 2 + 1, rows)
        return c

    def score_third(i, c):
        rows = pl.ds(pl.multiple_of(i * 512, 512), 512)
        st[rows, :] = st[rows, :] + score((1 - core) * 2, rows)
        return c

    lax.fori_loop(0, D // 512, score_half, 0)
    loop(NSH, lambda k: d_c2(k).wait())
    first, second_ = crecv[0], crecv[8]
    for i in range(1, 8):
        first = first + crecv[i]
        second_ = second_ + crecv[8 + i]
    codes = jnp.concatenate([first, second_], axis=1).astype(I32) - 1
    valid = codes >= 0
    rows_of = [jnp.broadcast_to(codes[s:s + 1, :], (8, 256)) for s in range(CAP)]
    sub_iota = iota((8, 256), 0)
    d_sib(0).wait()
    lax.fori_loop(0, D // 512, score_third, 0)
    d_sib(1).wait()

    def score_last(i, accs):
        base_row = pl.multiple_of(i * LAST, LAST)
        rows = pl.ds(base_row, LAST)
        vals = st[rows, :] + score((1 - core) * 2 + 1, rows)
        st[rows, :] = vals
        for j in range(LAST // 8):
            at = sub_iota + (base_row + j * 8)
            part = vals[j * 8:j * 8 + 8, :]
            accs = tuple(jnp.where(at == rows_of[s], part, a) for s, a in enumerate(accs))
        return accs

    accs = lax.fori_loop(0, D // LAST, score_last, tuple(jnp.zeros((8, 256), F32) for _ in range(CAP)))
    scores = jnp.concatenate([jnp.sum(a, axis=0, keepdims=True) for a in accs], axis=0) * (D ** -0.5)
    masked = jnp.where(valid, scores, NEG)
    m0 = jnp.max(masked, axis=0, keepdims=True)
    l0 = jnp.sum(jnp.where(valid, jnp.exp(masked - m0), 0.0), axis=0, keepdims=True)
    stat1[0:1, :] = m0
    stat1[1:2, :] = l0
    stat1[2:8, :] = jnp.zeros((6, 256), F32)
    stat1r[su] = stat1[...]

    def d_s1(k):
        return remote(stat1, stat1r.at[su], s1s.at[k], s1r.at[k], sub_peer(k))

    loop(NSU, lambda k: d_s1(k).start())

    qp = qall[0, :, 0:128]
    qp = jnp.where(iota((NQ, 128), 1) < PREFIX, qp.astype(F32), 0.0).astype(BF16)

    def prefix(i, top):
        rows = pl.ds(pl.multiple_of(i * 512, 512), 512)
        part = dot_nt(p_v[rows, 0:128], qp) * (PREFIX ** -0.5)
        cst[rows, :] = part
        return jnp.maximum(top, jnp.max(part.reshape(64, 8, 256), axis=0))

    top = lax.fori_loop(0, D // 512, prefix, jnp.full((8, 256), NEG, F32))
    cm = jnp.max(top, axis=0, keepdims=True)

    def expsum(i, tot):
        rows = pl.ds(pl.multiple_of(i * 64, 64), 64)
        return tot + jnp.sum(jnp.exp(cst[rows, :] - cm).reshape(8, 8, 256), axis=0)

    tot = lax.fori_loop(0, D // 64, expsum, jnp.zeros((8, 256), F32))
    cl = jnp.sum(tot, axis=0, keepdims=True)

    loop(NSU, lambda k: d_s1(k).wait())

    def join(buf, n, row):
        top = buf[0, row:row + 1, :]
        for i in range(1, n):
            top = jnp.maximum(top, buf[i, row:row + 1, :])
        total = jnp.zeros((1, 256), F32)
        for i in range(n):
            total = total + buf[i, row + 1:row + 2, :] * jnp.exp(buf[i, row:row + 1, :] - top)
        return top, total

    m1, l1 = join(stat1r, NSU, 0)
    stat2[0:1, :] = m1
    stat2[1:2, :] = l1
    stat2[2:3, :] = cm
    stat2[3:4, :] = cl
    stat2[4:8, :] = jnp.zeros((4, 256), F32)
    stat2r[sh] = stat2[...]

    def d_s2(k):
        return remote(stat2, stat2r.at[sh], s2s.at[k], s2r.at[k], shard_peer(k))

    loop(NSH, lambda k: d_s2(k).start())

    colt[:, 0:8] = codes.astype(F32).T
    colt[:, 8:16] = jnp.broadcast_to(m0, (8, 256)).T
    times = jnp.zeros((CAP, 256), F32)
    for s in range(CAP):
        times = times + jnp.where(codes == rows_of[s], 1.0, 0.0)
    colt[:, 16:24] = times.T

    def flip(i, c):
        rows = pl.ds(pl.multiple_of(i * 256, 256), 256)
        grown[:, rows] = st[rows, :].T
        return c

    lax.fori_loop(0, D // 256, flip, 0)

    def tally(i, c):
        rows = pl.ds(pl.multiple_of(i * 16, 16), 16)
        ct = colt[rows, 0:8].astype(I32)
        top = colt[rows, 8:9]
        ti = colt[rows, 16:24]
        for g in range(4):
            cols = iota((16, 512), 1) + g * 512
            here = slice(g * 512, (g + 1) * 512)
            val = jnp.zeros((16, 512), F32)
            for s in range(CAP):
                val = jnp.where(cols == ct[:, s:s + 1], ti[:, s:s + 1], val)
            count[rows, here] = val
            grown[rows, here] = jnp.where(val > 0.0, jnp.exp(grown[rows, here] * (D ** -0.5) - top), 0.0)
        return c

    lax.fori_loop(0, NQ // 16, tally, 0)
    loop(NSH, lambda k: d_s2(k).wait())
    m2, l2 = join(stat2r, NSH, 0)
    cm2, cl2 = join(stat2r, NSH, 2)

    scale = jnp.exp(m0 - m2) / l2
    probs = jnp.where(valid, jnp.exp(masked - m0), 0.0) * scale
    psend[0] = probs[:, 0:128]
    psend[1] = probs[:, 128:256]
    prtile[sh] = psend[sh // 8]

    def d_ps(k):
        return remote(psend.at[(sh ^ k) // 8], prtile.at[sh], ps_s.at[k], ps_r.at[k], shard_peer(k))

    loop(NSH, lambda k: d_ps(k).start())

    colt[:, 16:24] = jnp.broadcast_to(scale, (8, 256)).T

    def spread(i, c):
        rows = pl.ds(pl.multiple_of(i * 16, 16), 16)
        lows = pl.ds(pl.multiple_of(NQ + i * 16, 16), 16)
        f = colt[rows, 16:17]
        val = (grown[rows, :] * f).astype(BF16).astype(F32) * count[rows, :]
        hi = val.astype(BF16)
        whl[rows, :] = hi
        whl[lows, :] = (val - hi.astype(F32)).astype(BF16)
        return c

    lax.fori_loop(0, NQ // 16, spread, 0)

    def d_a(j):
        return remote(pool.at[j, 1 - core], ra.at[j], as_.at[j], ar_.at[j], sub_peer(1))

    def d_b(j, k):
        return remote(pool.at[j, core, pl.ds((a1 ^ k) * 4, 4)], rb.at[j, pl.ds(k * 4, 4)],
                      bs_.at[j, k], br_.at[j, k], shard_peer(k * step1))

    def d_e(j, k):
        return remote(rb.at[j, a2 ^ k], re.at[j, k], es_.at[j, k], er_.at[j, k], shard_peer(k * step2))

    def multiply(j):
        cols = slice(j * CW, (j + 1) * CW)
        part = jnp.dot(whl[...], p_v[:, cols], preferred_element_type=F32)
        part = part[:NQ] + part[NQ:]
        for i in range(NSH):
            for c in range(2):
                pool[j, c, i if c == 0 else (i % 4) * 4 + i // 4] = part[i * 16 + c * 8:i * 16 + c * 8 + 8, :]
        d_a(j).start()

    def forward(j):
        d_a(j).wait()
        for i in range(NSH):
            pool[j, core, i] = pool[j, core, i] + ra[j, i]
        loop(4, lambda k: d_b(j, k).start())

    def second(j):
        loop(4, lambda k: d_b(j, k).wait())
        for i in range(4):
            rb[j, i] = pool[j, core, a1 * 4 + i] + rb[j, 4 + i] + rb[j, 8 + i] + rb[j, 12 + i]
        loop(4, lambda k: d_e(j, k).start())

    def third(j):
        loop(4, lambda k: d_e(j, k).wait())
        tile = rb[j, a2] + re[j, 1] + re[j, 2] + re[j, 3]
        for t in range(2):
            for i in range(4):
                zsend[i, t * 8 + j:t * 8 + j + 1, :] = tile[t * 4 + i:t * 4 + i + 1, :]

    def at_once(j):
        loop(4, lambda k: d_b(j, k).wait())
        for i in range(4):
            tile = pool[j, core, a1 * 4 + i] + rb[j, 4 + i] + rb[j, 8 + i] + rb[j, 12 + i]
            for t in range(2):
                for e in range(4):
                    for g in range(CW // 128):
                        row = ((j - TWO_HOP) * 2 + t) * (CW // 128) + g
                        lsend[i * 4 + e, row:row + 1, :] = tile[t * 4 + e:t * 4 + e + 1, g * 128:(g + 1) * 128]

    def d_l(k):
        return remote(lsend.at[(a2 ^ (k // 4)) * 4 + (z ^ (k % 4))], lrecv.at[a2 * 4 + z], ls_.at[k], lr_.at[k],
                      (sh ^ ((k // 4) * step2), su ^ (2 * (k % 4))))

    multiply(0)
    multiply(1)
    forward(0)
    multiply(2)
    forward(1)
    multiply(3)
    forward(2)
    second(0)
    forward(3)
    second(1)

    loop(NSH, lambda k: d_ps(k).wait())
    outs = [[jnp.zeros((8, 128), F32) for _ in range(2)] for _ in range(NSU)]
    for h in range(NSH):
        mine = pltpu.roll(prtile[h], 128 - base, 1)
        here = lane == su * NSH + h
        for d in range(NSU):
            for t in range(2):
                col = (d % 2) * 8 + t * 4 + d // 2
                outs[d][t] = jnp.where(here, jnp.broadcast_to(mine[:, col:col + 1], (8, 128)), outs[d][t])
    coarse = jnp.concatenate([cm2[:, 0:128], cm2[:, 128:256], cl2[:, 0:128], cl2[:, 128:256],
                              jnp.zeros((4, 128), F32)], axis=0)
    for d in range(NSU):
        for t in range(2):
            pusend[d, t * 8:t * 8 + 8, :] = outs[d][t]
        pusend[d, 16:24, :] = coarse
    purecv[su] = pusend[su]

    def d_pu(k):
        return remote(pusend.at[su ^ k], purecv.at[su], pu_s.at[k], pu_r.at[k], sub_peer(k))

    loop(NSU, lambda k: d_pu(k).start())

    second(2)
    third(0)
    third(1)
    at_once(3)
    lrecv[a2 * 4 + z] = lsend[a2 * 4 + z]
    loop(NSH, lambda k: d_l(k).start())
    third(2)
    for i in range(4):
        zsend[i, TWO_HOP:8, :] = jnp.zeros((8 - TWO_HOP, CW), F32)
        zsend[i, 8 + TWO_HOP:16, :] = jnp.zeros((8 - TWO_HOP, CW), F32)
    zr[z] = zsend[z]

    def d_z(k):
        return remote(zsend.at[z ^ k], zr.at[z], zs_.at[k], zr_.at[k], sub_peer(2 * k))

    loop(4, lambda k: d_z(k).start())

    loop(NSU, lambda k: d_pu(k).wait())
    for t in range(2):
        p = purecv[0, t * 8:t * 8 + 8, :]
        for i in range(1, NSU):
            p = p + purecv[i, t * 8:t * 8 + 8, :]
        p1 = p.astype(BF16)
        rest = p - p1.astype(F32)
        p2 = rest.astype(BF16)
        p3 = (rest - p2.astype(F32)).astype(BF16)
        y = jnp.dot(jnp.concatenate([p1.astype(F32), p2.astype(F32), p3.astype(F32)], axis=0).astype(BF16),
                    onehots[t], preferred_element_type=F32)
        y = y[0:8] + y[8:16] + y[16:24]
        row = jnp.sum(jnp.where(iota((CAP, 256), 0).astype(F32) == ranks[t], y, 0.0), axis=0, keepdims=True)
        probs_ref[t:t + 1, :] = row[:, :CANDS]
    top = purecv[0, 16:18, :]
    for i in range(1, NSU):
        top = jnp.maximum(top, purecv[i, 16:18, :])
    total = jnp.zeros((2, 128), F32)
    for i in range(NSU):
        total = total + purecv[i, 18:20, :] * jnp.exp(purecv[i, 16:18, :] - top)
    lse = top + jnp.log(total)
    spot = iota((2, 128), 0) * 128 + iota((2, 128), 1)
    for t in range(2):
        mine = jnp.where(spot == sh * 16 + core * 8 + t * 4 + z, lse, 0.0)
        lse_ref[0:1, t:t + 1] = jnp.sum(mine, keepdims=True)

    loop(4, lambda k: d_z(k).wait())
    final = zr[0] + zr[1] + zr[2] + zr[3]
    for t in range(2):
        for j in range(TWO_HOP):
            out_ref[t:t + 1, j * CW:(j + 1) * CW] = final[t * 8 + j:t * 8 + j + 1, :].astype(BF16)
    loop(NSH, lambda k: d_l(k).wait())
    final = lrecv[0]
    for i in range(1, NSH):
        final = final + lrecv[i]
    for j in range(TWO_HOP, CHUNKS):
        for t in range(2):
            for g in range(CW // 128):
                row = ((j - TWO_HOP) * 2 + t) * (CW // 128) + g
                out_ref[t:t + 1, j * CW + g * 128:j * CW + (g + 1) * 128] = final[row:row + 1, :].astype(BF16)


def shards(queries, passages, candidates):
    vmem = pl.BlockSpec(memory_space=pltpu.VMEM)
    V, DMA = pltpu.VMEM, pltpu.SemaphoreType.DMA
    lse, probs, pooled = pl.pallas_call(
        kernel,
        name="retrieve",
        out_shape=(
            jax.ShapeDtypeStruct((1, 2), F32),
            jax.ShapeDtypeStruct((2, CANDS), F32),
            jax.ShapeDtypeStruct((2, D), BF16),
        ),
        in_specs=[vmem, vmem, pl.BlockSpec(memory_space=pl.ANY)],
        out_specs=(vmem, vmem, vmem),
        scratch_shapes=[
            V((D, D), BF16), V((2, CANDS), I32), V((2, D), BF16), V((2, 256), I32), V((16, 256), F32), V((16, 256), BF16), V((16, 128), F32),
            V((NSU, 16, 256), BF16), V((NSU, 16, 128), F32), V((16, D), F32), V((4, 16, QW), BF16),
            V((4, NQ, QW), BF16), V((NSH, 8, 128), F32), V((NSH, 8, 128), F32),
            V((D, NQ), F32), V((D, NQ), F32),
            V((8, 256), F32), V((NSU, 8, 256), F32), V((8, 256), F32), V((NSH, 8, 256), F32),
            V((NQ, 128), F32), V((NQ, D), F32), V((NQ, D), F32), V((2 * NQ, D), BF16),
            V((CHUNKS, 2, NSH, 8, CW), F32), V((CHUNKS, NSH, 8, CW), F32), V((CHUNKS, NSH, 8, CW), F32),
            V((CHUNKS, 4, 8, CW), F32),
            V((4, 16, CW), F32), V((4, 16, CW), F32), V((NSH, 8, 128), F32), V((NSH, 8, 128), F32), V((2, 8, 128), F32), V((NSH, 8, 128), F32),
            V((NSU, 24, 128), F32), V((NSU, 24, 128), F32),
            DMA(()), DMA((2,)),
            DMA((NSU,)), DMA((NSU,)), DMA((NSU,)), DMA((NSU,)),
            DMA((4,)), DMA((4,)), DMA((4, 4)), DMA((4, 4)), DMA((NSH,)), DMA((NSH,)), DMA((2,)), DMA((2,)),
            DMA((NSU,)), DMA((NSU,)), DMA((NSH,)), DMA((NSH,)),
            DMA((NSH,)), DMA((NSH,)), DMA((NSU,)), DMA((NSU,)),
            DMA((CHUNKS,)), DMA((CHUNKS,)), DMA((CHUNKS, 4)), DMA((CHUNKS, 4)), DMA((CHUNKS, 4)), DMA((CHUNKS, 4)),
            DMA((4,)), DMA((4,)), DMA((NSH,)), DMA((NSH,)),
        ],
        compiler_params=pltpu.CompilerParams(
            collective_id=0, has_side_effects=True, vmem_limit_bytes=50 * 1024 * 1024
        ),
    )(candidates, queries, passages)
    return lse.reshape(2), probs, pooled


def solution(mesh):
    spec = P(("shard", "sub"), None)
    return jax.shard_map(shards, mesh=mesh, in_specs=(spec, spec, spec),
                         out_specs=(P(("shard", "sub")), spec, spec), check_vma=False)
```

```python
import jax
import jax.numpy as jnp
from jax import lax
from jax.experimental import pallas as pl
from jax.experimental.pallas import tpu as pltpu
from jax.sharding import PartitionSpec as P

NSH, NSU = 16, 8
NDEV = NSH * NSU
D = 2048
QW = D // 4
LAST = 256
PREFIX = 64
CANDS = 200
CAP = 8
NQ = 256
CHUNKS = 4
CW = D // CHUNKS
TWO_HOP = CHUNKS - 1
NEG = -3.0e38
MESH = pl.DeviceIdType.MESH
F32, BF16, I32 = jnp.float32, jnp.bfloat16, jnp.int32


def iota(shape, dim):
    return lax.broadcasted_iota(I32, shape, dim)


def dot_nt(a, b):
    return lax.dot_general(a, b, (((1,), (1,)), ((), ())), preferred_element_type=F32)


def kernel(cand_hbm, q_hbm, p_hbm, lse_ref, probs_ref, out_ref,
           p_v, cand_v, q_v, candp, qf, qsend, code, qbuf, cbuf, q16f, q16, qall, ctile, crecv,
           st, cst, stat1, stat1r, stat2, stat2r, colt, count, grown, whl,
           pool, ra, rb, re, zsend, zr, lsend, lrecv, psend, prtile, pusend, purecv,
           p_sem, in_sem, q1s, q1r, c1s, c1r, q2s, q2r, q3s, q3r, c2s, c2r, sibs, sibr,
           s1s, s1r, s2s, s2r, ps_s, ps_r, pu_s, pu_r, as_, ar_, bs_, br_, es_, er_, zs_, zr_, ls_, lr_):
    sh, su = lax.axis_index("shard"), lax.axis_index("sub")
    core, z = su % 2, su // 2
    y, x = sh // 4, sh % 4
    a1, a2 = y + core * (x - y), x + core * (y - x)
    step1, step2 = 4 - 3 * core, 1 + 3 * core

    def sub_peer(k):
        return (sh, su ^ k)

    def shard_peer(k):
        return (sh ^ k, su)

    barrier = pltpu.get_barrier_semaphore()

    def greet(k, c):
        pl.semaphore_signal(barrier, inc=1, device_id=shard_peer(k), device_id_type=MESH)
        return c

    def greet_sub(k, c):
        pl.semaphore_signal(barrier, inc=1, device_id=sub_peer(k), device_id_type=MESH)
        return c

    for k in (8, 2, 4, 12, 1, 3):
        greet(k, 0)
    for k in (4, 5, 2, 3, 6, 7, 1):
        greet_sub(k, 0)
    load_p = pltpu.make_async_copy(p_hbm, p_v, p_sem)
    load_p.start()

    def loop(n, fn):
        for k in range(1, n):
            fn(k)

    def remote(src, dst, s, r, peer):
        return pltpu.make_async_remote_copy(src_ref=src, dst_ref=dst, send_sem=s, recv_sem=r,
                                            device_id=peer, device_id_type=MESH)

    qs = q_hbm[...].astype(F32)
    for r in range(8):
        qf[2 * r:2 * r + 2, :] = qs[:, r * 256:(r + 1) * 256]
    qsend[...] = qf[...].astype(BF16)
    qbuf[su] = qsend[...]

    pl.semaphore_wait(barrier, 6 + 7)

    def d_q1(k):
        return remote(qsend, qbuf.at[su], q1s.at[k], q1r.at[k], sub_peer(k))

    def d_c1(k):
        return remote(code, cbuf.at[su], c1s.at[k], c1r.at[k], sub_peer(k))

    loop(NSU, lambda k: d_q1(k).start())

    candp[...] = jnp.full((2, 256), -1, I32)
    candp[:, :CANDS] = cand_hbm[...]
    upper = jnp.where(iota((256, 256), 0) <= iota((256, 256), 1), 1.0, 0.0).astype(BF16)
    onehots, ranks = [], []
    before = jnp.zeros((128, 1), F32)
    for t in range(2):
        ids = candp[t:t + 1, :]
        dev = ids // D
        place = jnp.where(ids >= 0, (dev % NSU) * NSH + dev // NSU, -1)
        local = ids - dev * D + 1
        oh = jnp.where(iota((128, 256), 0) == place, 1.0, 0.0)
        ohb = oh.astype(BF16)
        cum = jnp.dot(ohb, upper, preferred_element_type=F32) + before
        rank = jnp.sum(oh * cum, axis=0, keepdims=True) - 1.0
        before = cum[:, 255:256]
        at = iota((CAP, 256), 0).astype(F32) == rank
        high = jnp.where(at, (local // 64).astype(F32), 0.0)
        low = jnp.where(at, (local % 64).astype(F32), 0.0)
        parts = dot_nt(jnp.concatenate([high, low], axis=0).astype(BF16), ohb)
        code[t * 8:t * 8 + 8, :] = parts[:8] * 64.0 + parts[8:]
        onehots.append(ohb)
        ranks.append(rank)

    cbuf[su] = code[...]
    loop(NSU, lambda k: d_c1(k).start())
    loop(NSU, lambda k: d_q1(k).wait())
    for i in range(NSU):
        block = qbuf[i].astype(F32)
        for r in range(8):
            for t in range(2):
                row = (i % 2) * 8 + t * 4 + i // 2
                q16f[row:row + 1, r * 256:(r + 1) * 256] = block[2 * r + t:2 * r + t + 1, :]
    for h in range(4):
        q16[h] = q16f[:, h * QW:(h + 1) * QW].astype(BF16)
    for c in range(2):
        qall[core * 2 + c, pl.ds(pl.multiple_of(sh * 16, 16), 16), :] = q16[core * 2 + c]

    def q_block(j):
        return qall.at[pl.ds(core * 2, 2), pl.ds(pl.multiple_of((sh ^ (j * step1)) * 16, 16), 16)]

    def d_q2(k):
        return remote(q_block(0), q_block(0), q2s.at[k], q2r.at[k], shard_peer(k * step1))

    def d_q3(j, k):
        return remote(q_block(j), q_block(j), q3s.at[j, k], q3r.at[j, k], shard_peer(k * step2))

    def d_c2(k):
        return remote(ctile.at[sh ^ k], crecv.at[sh], c2s.at[k], c2r.at[k], shard_peer(k))

    loop(4, lambda k: d_q2(k).start())
    loop(4, lambda k: d_q3(0, k).start())
    loop(NSU, lambda k: d_c1(k).wait())
    lane = iota((8, 128), 1)
    base = (sh % 8) * 16
    tiles = [jnp.zeros((8, 128), F32) for _ in range(NSH)]
    for i in range(NSU):
        for t in range(2):
            mine = pltpu.roll(cbuf[i, t * 8:t * 8 + 8, :], (NSU - su) * NSH, 1)
            here = lane == base + ((i % 2) * 8 + t * 4 + i // 2)
            for j in range(NSH):
                tiles[j] = jnp.where(here, jnp.broadcast_to(mine[:, j:j + 1], (8, 128)), tiles[j])
    for j in range(NSH):
        ctile[j] = tiles[j]
    crecv[sh] = ctile[sh]

    for j in range(1, 4):
        d_q2(j).wait()
        loop(4, lambda k: d_q3(j, k).start())

    loop(NSH, lambda k: d_c2(k).start())
    for j in range(4):
        loop(4, lambda k: d_q3(j, k).wait())
    def d_sib(c):
        part = qall.at[core * 2 + c]
        return remote(part, part, sibs.at[c], sibr.at[c], sub_peer(1))

    d_sib(0).start()
    d_sib(1).start()
    load_p.wait()

    def score(h, rows):
        cols = pl.ds(pl.multiple_of(h * QW, QW), QW)
        return dot_nt(p_v[rows, cols], qall[h])

    def score_half(i, c):
        rows = pl.ds(pl.multiple_of(i * 512, 512), 512)
        st[rows, :] = score(core * 2, rows) + score(core * 2 + 1, rows)
        return c

    def score_third(i, c):
        rows = pl.ds(pl.multiple_of(i * 512, 512), 512)
        st[rows, :] = st[rows, :] + score((1 - core) * 2, rows)
        return c

    lax.fori_loop(0, D // 512, score_half, 0)
    loop(NSH, lambda k: d_c2(k).wait())
    first, second_ = crecv[0], crecv[8]
    for i in range(1, 8):
        first = first + crecv[i]
        second_ = second_ + crecv[8 + i]
    codes = jnp.concatenate([first, second_], axis=1).astype(I32) - 1
    valid = codes >= 0
    rows_of = [jnp.broadcast_to(codes[s:s + 1, :], (8, 256)) for s in range(CAP)]
    sub_iota = iota((8, 256), 0)
    d_sib(0).wait()
    lax.fori_loop(0, D // 512, score_third, 0)
    d_sib(1).wait()

    def score_last(i, accs):
        base_row = pl.multiple_of(i * LAST, LAST)
        rows = pl.ds(base_row, LAST)
        vals = st[rows, :] + score((1 - core) * 2 + 1, rows)
        st[rows, :] = vals
        for j in range(LAST // 8):
            at = sub_iota + (base_row + j * 8)
            part = vals[j * 8:j * 8 + 8, :]
            accs = tuple(jnp.where(at == rows_of[s], part, a) for s, a in enumerate(accs))
        return accs

    accs = lax.fori_loop(0, D // LAST, score_last, tuple(jnp.zeros((8, 256), F32) for _ in range(CAP)))
    scores = jnp.concatenate([jnp.sum(a, axis=0, keepdims=True) for a in accs], axis=0) * (D ** -0.5)
    masked = jnp.where(valid, scores, NEG)
    m0 = jnp.max(masked, axis=0, keepdims=True)
    l0 = jnp.sum(jnp.where(valid, jnp.exp(masked - m0), 0.0), axis=0, keepdims=True)
    def fold(v):
        return jnp.concatenate([v[:, 0:128], v[:, 128:256]], axis=0)

    def unfold(v):
        return jnp.concatenate([v[0:1, :], v[1:2, :]], axis=1)

    stat1[0:2, :] = fold(m0)
    stat1[2:4, :] = fold(l0)
    stat1[4:8, :] = jnp.zeros((4, 128), F32)
    stat1r[su] = stat1[...]

    def d_s1(k):
        return remote(stat1, stat1r.at[su], s1s.at[k], s1r.at[k], sub_peer(k))

    loop(NSU, lambda k: d_s1(k).start())

    qp = qall[0, :, 0:128]
    qp = jnp.where(iota((NQ, 128), 1) < PREFIX, qp.astype(F32), 0.0).astype(BF16)

    def prefix(i, top):
        rows = pl.ds(pl.multiple_of(i * 512, 512), 512)
        part = dot_nt(p_v[rows, 0:128], qp) * (PREFIX ** -0.5)
        cst[rows, :] = part
        return jnp.maximum(top, jnp.max(part.reshape(64, 8, 256), axis=0))

    top = lax.fori_loop(0, D // 512, prefix, jnp.full((8, 256), NEG, F32))
    cm = jnp.max(top, axis=0, keepdims=True)

    def expsum(i, tot):
        rows = pl.ds(pl.multiple_of(i * 64, 64), 64)
        return tot + jnp.sum(jnp.exp(cst[rows, :] - cm).reshape(8, 8, 256), axis=0)

    tot = lax.fori_loop(0, D // 64, expsum, jnp.zeros((8, 256), F32))
    cl = jnp.sum(tot, axis=0, keepdims=True)

    loop(NSU, lambda k: d_s1(k).wait())

    def join(buf, n, row):
        top = buf[0, row:row + 2, :]
        for i in range(1, n):
            top = jnp.maximum(top, buf[i, row:row + 2, :])
        total = jnp.zeros((2, 128), F32)
        for i in range(n):
            total = total + buf[i, row + 2:row + 4, :] * jnp.exp(buf[i, row:row + 2, :] - top)
        return top, total

    m1, l1 = join(stat1r, NSU, 0)
    stat2[0:2, :] = m1
    stat2[2:4, :] = l1
    stat2[4:6, :] = fold(cm)
    stat2[6:8, :] = fold(cl)
    stat2r[sh] = stat2[...]

    def d_s2(k):
        return remote(stat2, stat2r.at[sh], s2s.at[k], s2r.at[k], shard_peer(k))

    loop(NSH, lambda k: d_s2(k).start())

    colt[:, 0:8] = codes.astype(F32).T
    colt[:, 8:16] = jnp.broadcast_to(m0, (8, 256)).T
    times = jnp.zeros((CAP, 256), F32)
    for s in range(CAP):
        times = times + jnp.where(codes == rows_of[s], 1.0, 0.0)
    colt[:, 16:24] = times.T

    def flip(i, c):
        rows = pl.ds(pl.multiple_of(i * 256, 256), 256)
        grown[:, rows] = st[rows, :].T
        return c

    lax.fori_loop(0, D // 256, flip, 0)

    def tally(i, c):
        rows = pl.ds(pl.multiple_of(i * 16, 16), 16)
        ct = colt[rows, 0:8].astype(I32)
        top = colt[rows, 8:9]
        ti = colt[rows, 16:24]
        for g in range(4):
            cols = iota((16, 512), 1) + g * 512
            here = slice(g * 512, (g + 1) * 512)
            val = jnp.zeros((16, 512), F32)
            for s in range(CAP):
                val = jnp.where(cols == ct[:, s:s + 1], ti[:, s:s + 1], val)
            count[rows, here] = val
            grown[rows, here] = jnp.where(val > 0.0, jnp.exp(grown[rows, here] * (D ** -0.5) - top), 0.0)
        return c

    lax.fori_loop(0, NQ // 16, tally, 0)
    loop(NSH, lambda k: d_s2(k).wait())
    m2, l2 = (unfold(v) for v in join(stat2r, NSH, 0))
    cm2, cl2 = join(stat2r, NSH, 4)

    scale = jnp.exp(m0 - m2) / l2
    probs = jnp.where(valid, jnp.exp(masked - m0), 0.0) * scale
    psend[0] = probs[:, 0:128]
    psend[1] = probs[:, 128:256]
    prtile[sh] = psend[sh // 8]

    def d_ps(k):
        return remote(psend.at[(sh ^ k) // 8], prtile.at[sh], ps_s.at[k], ps_r.at[k], shard_peer(k))

    loop(NSH, lambda k: d_ps(k).start())

    colt[:, 16:24] = jnp.broadcast_to(scale, (8, 256)).T

    def spread(i, c):
        rows = pl.ds(pl.multiple_of(i * 16, 16), 16)
        lows = pl.ds(pl.multiple_of(NQ + i * 16, 16), 16)
        f = colt[rows, 16:17]
        val = (grown[rows, :] * f).astype(BF16).astype(F32) * count[rows, :]
        hi = val.astype(BF16)
        whl[rows, :] = hi
        whl[lows, :] = (val - hi.astype(F32)).astype(BF16)
        return c

    lax.fori_loop(0, NQ // 16, spread, 0)

    def d_a(j):
        return remote(pool.at[j, 1 - core], ra.at[j], as_.at[j], ar_.at[j], sub_peer(1))

    def d_b(j, k):
        return remote(pool.at[j, core, pl.ds((a1 ^ k) * 4, 4)], rb.at[j, pl.ds(k * 4, 4)],
                      bs_.at[j, k], br_.at[j, k], shard_peer(k * step1))

    def d_e(j, k):
        return remote(rb.at[j, a2 ^ k], re.at[j, k], es_.at[j, k], er_.at[j, k], shard_peer(k * step2))

    def multiply(j):
        cols = slice(j * CW, (j + 1) * CW)
        part = jnp.dot(whl[...], p_v[:, cols], preferred_element_type=F32)
        part = part[:NQ] + part[NQ:]
        for i in range(NSH):
            for c in range(2):
                pool[j, c, i if c == 0 else (i % 4) * 4 + i // 4] = part[i * 16 + c * 8:i * 16 + c * 8 + 8, :]
        d_a(j).start()

    def forward(j):
        d_a(j).wait()
        for i in range(NSH):
            pool[j, core, i] = pool[j, core, i] + ra[j, i]
        loop(4, lambda k: d_b(j, k).start())

    def second(j):
        loop(4, lambda k: d_b(j, k).wait())
        for i in range(4):
            rb[j, i] = pool[j, core, a1 * 4 + i] + rb[j, 4 + i] + rb[j, 8 + i] + rb[j, 12 + i]
        loop(4, lambda k: d_e(j, k).start())

    def third(j):
        loop(4, lambda k: d_e(j, k).wait())
        tile = rb[j, a2] + re[j, 1] + re[j, 2] + re[j, 3]
        for t in range(2):
            for i in range(4):
                zsend[i, t * 8 + j:t * 8 + j + 1, :] = tile[t * 4 + i:t * 4 + i + 1, :]

    def at_once(j):
        loop(4, lambda k: d_b(j, k).wait())
        for i in range(4):
            tile = pool[j, core, a1 * 4 + i] + rb[j, 4 + i] + rb[j, 8 + i] + rb[j, 12 + i]
            for t in range(2):
                for e in range(4):
                    for g in range(CW // 128):
                        row = ((j - TWO_HOP) * 2 + t) * (CW // 128) + g
                        lsend[i * 4 + e, row:row + 1, :] = tile[t * 4 + e:t * 4 + e + 1, g * 128:(g + 1) * 128]

    def d_l(k):
        return remote(lsend.at[(a2 ^ (k // 4)) * 4 + (z ^ (k % 4))], lrecv.at[a2 * 4 + z], ls_.at[k], lr_.at[k],
                      (sh ^ ((k // 4) * step2), su ^ (2 * (k % 4))))

    multiply(0)
    multiply(1)
    forward(0)
    multiply(2)
    forward(1)
    multiply(3)
    forward(2)
    second(0)
    forward(3)
    second(1)

    loop(NSH, lambda k: d_ps(k).wait())
    outs = [[jnp.zeros((8, 128), F32) for _ in range(2)] for _ in range(NSU)]
    for h in range(NSH):
        mine = pltpu.roll(prtile[h], 128 - base, 1)
        here = lane == su * NSH + h
        for d in range(NSU):
            for t in range(2):
                col = (d % 2) * 8 + t * 4 + d // 2
                outs[d][t] = jnp.where(here, jnp.broadcast_to(mine[:, col:col + 1], (8, 128)), outs[d][t])
    coarse = jnp.concatenate([cm2, cl2, jnp.zeros((4, 128), F32)], axis=0)
    for d in range(NSU):
        for t in range(2):
            pusend[d, t * 8:t * 8 + 8, :] = outs[d][t]
        pusend[d, 16:24, :] = coarse
    purecv[su] = pusend[su]

    def d_pu(k):
        return remote(pusend.at[su ^ k], purecv.at[su], pu_s.at[k], pu_r.at[k], sub_peer(k))

    loop(NSU, lambda k: d_pu(k).start())

    second(2)
    third(0)
    third(1)
    at_once(3)
    lrecv[a2 * 4 + z] = lsend[a2 * 4 + z]
    loop(NSH, lambda k: d_l(k).start())
    third(2)
    for i in range(4):
        zsend[i, TWO_HOP:8, :] = jnp.zeros((8 - TWO_HOP, CW), F32)
        zsend[i, 8 + TWO_HOP:16, :] = jnp.zeros((8 - TWO_HOP, CW), F32)
    zr[z] = zsend[z]

    def d_z(k):
        return remote(zsend.at[z ^ k], zr.at[z], zs_.at[k], zr_.at[k], sub_peer(2 * k))

    loop(4, lambda k: d_z(k).start())

    loop(NSU, lambda k: d_pu(k).wait())
    for t in range(2):
        p = purecv[0, t * 8:t * 8 + 8, :]
        for i in range(1, NSU):
            p = p + purecv[i, t * 8:t * 8 + 8, :]
        p1 = p.astype(BF16)
        rest = p - p1.astype(F32)
        p2 = rest.astype(BF16)
        p3 = (rest - p2.astype(F32)).astype(BF16)
        y = jnp.dot(jnp.concatenate([p1.astype(F32), p2.astype(F32), p3.astype(F32)], axis=0).astype(BF16),
                    onehots[t], preferred_element_type=F32)
        y = y[0:8] + y[8:16] + y[16:24]
        row = jnp.sum(jnp.where(iota((CAP, 256), 0).astype(F32) == ranks[t], y, 0.0), axis=0, keepdims=True)
        probs_ref[t:t + 1, :] = row[:, :CANDS]
    top = purecv[0, 16:18, :]
    for i in range(1, NSU):
        top = jnp.maximum(top, purecv[i, 16:18, :])
    total = jnp.zeros((2, 128), F32)
    for i in range(NSU):
        total = total + purecv[i, 18:20, :] * jnp.exp(purecv[i, 16:18, :] - top)
    lse = top + jnp.log(total)
    spot = iota((2, 128), 0) * 128 + iota((2, 128), 1)
    for t in range(2):
        mine = jnp.where(spot == sh * 16 + core * 8 + t * 4 + z, lse, 0.0)
        lse_ref[0:1, t:t + 1] = jnp.sum(mine, keepdims=True)

    loop(4, lambda k: d_z(k).wait())
    final = zr[0] + zr[1] + zr[2] + zr[3]
    for t in range(2):
        for j in range(TWO_HOP):
            out_ref[t:t + 1, j * CW:(j + 1) * CW] = final[t * 8 + j:t * 8 + j + 1, :].astype(BF16)
    loop(NSH, lambda k: d_l(k).wait())
    final = lrecv[0]
    for i in range(1, NSH):
        final = final + lrecv[i]
    for j in range(TWO_HOP, CHUNKS):
        for t in range(2):
            for g in range(CW // 128):
                row = ((j - TWO_HOP) * 2 + t) * (CW // 128) + g
                out_ref[t:t + 1, j * CW + g * 128:j * CW + (g + 1) * 128] = final[row:row + 1, :].astype(BF16)


def shards(queries, passages, candidates):
    vmem = pl.BlockSpec(memory_space=pltpu.VMEM)
    V, DMA = pltpu.VMEM, pltpu.SemaphoreType.DMA
    lse, probs, pooled = pl.pallas_call(
        kernel,
        name="retrieve",
        out_shape=(
            jax.ShapeDtypeStruct((1, 2), F32),
            jax.ShapeDtypeStruct((2, CANDS), F32),
            jax.ShapeDtypeStruct((2, D), BF16),
        ),
        in_specs=[vmem, vmem, pl.BlockSpec(memory_space=pl.ANY)],
        out_specs=(vmem, vmem, vmem),
        scratch_shapes=[
            V((D, D), BF16), V((2, CANDS), I32), V((2, D), BF16), V((2, 256), I32), V((16, 256), F32), V((16, 256), BF16), V((16, 128), F32),
            V((NSU, 16, 256), BF16), V((NSU, 16, 128), F32), V((16, D), F32), V((4, 16, QW), BF16),
            V((4, NQ, QW), BF16), V((NSH, 8, 128), F32), V((NSH, 8, 128), F32),
            V((D, NQ), F32), V((D, NQ), F32),
            V((8, 128), F32), V((NSU, 8, 128), F32), V((8, 128), F32), V((NSH, 8, 128), F32),
            V((NQ, 128), F32), V((NQ, D), F32), V((NQ, D), F32), V((2 * NQ, D), BF16),
            V((CHUNKS, 2, NSH, 8, CW), F32), V((CHUNKS, NSH, 8, CW), F32), V((CHUNKS, NSH, 8, CW), F32),
            V((CHUNKS, 4, 8, CW), F32),
            V((4, 16, CW), F32), V((4, 16, CW), F32), V((NSH, 8, 128), F32), V((NSH, 8, 128), F32), V((2, 8, 128), F32), V((NSH, 8, 128), F32),
            V((NSU, 24, 128), F32), V((NSU, 24, 128), F32),
            DMA(()), DMA((2,)),
            DMA((NSU,)), DMA((NSU,)), DMA((NSU,)), DMA((NSU,)),
            DMA((4,)), DMA((4,)), DMA((4, 4)), DMA((4, 4)), DMA((NSH,)), DMA((NSH,)), DMA((2,)), DMA((2,)),
            DMA((NSU,)), DMA((NSU,)), DMA((NSH,)), DMA((NSH,)),
            DMA((NSH,)), DMA((NSH,)), DMA((NSU,)), DMA((NSU,)),
            DMA((CHUNKS,)), DMA((CHUNKS,)), DMA((CHUNKS, 4)), DMA((CHUNKS, 4)), DMA((CHUNKS, 4)), DMA((CHUNKS, 4)),
            DMA((4,)), DMA((4,)), DMA((NSH,)), DMA((NSH,)),
        ],
        compiler_params=pltpu.CompilerParams(
            collective_id=0, has_side_effects=True, vmem_limit_bytes=50 * 1024 * 1024
        ),
    )(candidates, queries, passages)
    return lse.reshape(2), probs, pooled


def solution(mesh):
    spec = P(("shard", "sub"), None)
    return jax.shard_map(shards, mesh=mesh, in_specs=(spec, spec, spec),
                         out_specs=(P(("shard", "sub")), spec, spec), check_vma=False)
```

```python
import jax
import jax.numpy as jnp
from jax import lax
from jax.experimental import pallas as pl
from jax.experimental.pallas import tpu as pltpu
from jax.sharding import PartitionSpec as P

NSH, NSU = 16, 8
NDEV = NSH * NSU
D = 2048
QW = D // 4
LAST = 512
PREFIX = 64
CANDS = 200
CAP = 8
NQ = 256
CHUNKS = 4
CW = D // CHUNKS
TWO_HOP = CHUNKS - 2
NEG = -3.0e38
MESH = pl.DeviceIdType.MESH
F32, BF16, I32 = jnp.float32, jnp.bfloat16, jnp.int32


def iota(shape, dim):
    return lax.broadcasted_iota(I32, shape, dim)


def dot_nt(a, b):
    return lax.dot_general(a, b, (((1,), (1,)), ((), ())), preferred_element_type=F32)


def kernel(cand_hbm, q_hbm, p_hbm, lse_ref, probs_ref, out_ref,
           p_v, cand_v, q_v, candp, qf, qsend, code, qbuf, cbuf, q16f, q16, qall, ctile, crecv,
           st, cst, stat1, stat1r, stat2, stat2r, colt, count, grown, whl,
           pool, ra, rb, re, zsend, zr, lsend, lrecv, psend, prtile, pusend, purecv,
           p_sem, in_sem, q1s, q1r, c1s, c1r, q2s, q2r, q3s, q3r, c2s, c2r, sibs, sibr,
           s1s, s1r, s2s, s2r, ps_s, ps_r, pu_s, pu_r, as_, ar_, bs_, br_, es_, er_, zs_, zr_, ls_, lr_):
    sh, su = lax.axis_index("shard"), lax.axis_index("sub")
    core, z = su % 2, su // 2
    y, x = sh // 4, sh % 4
    a1, a2 = y + core * (x - y), x + core * (y - x)
    step1, step2 = 4 - 3 * core, 1 + 3 * core

    def sub_peer(k):
        return (sh, su ^ k)

    def shard_peer(k):
        return (sh ^ k, su)

    barrier = pltpu.get_barrier_semaphore()

    def greet(k, c):
        pl.semaphore_signal(barrier, inc=1, device_id=shard_peer(k), device_id_type=MESH)
        return c

    def greet_sub(k, c):
        pl.semaphore_signal(barrier, inc=1, device_id=sub_peer(k), device_id_type=MESH)
        return c

    for k in (8, 2, 4, 12, 1, 3):
        greet(k, 0)
    for k in (4, 5, 2, 3, 6, 7, 1):
        greet_sub(k, 0)
    load_p = pltpu.make_async_copy(p_hbm, p_v, p_sem)
    load_p.start()

    def loop(n, fn):
        for k in range(1, n):
            fn(k)

    def remote(src, dst, s, r, peer):
        return pltpu.make_async_remote_copy(src_ref=src, dst_ref=dst, send_sem=s, recv_sem=r,
                                            device_id=peer, device_id_type=MESH)

    qs = q_hbm[...].astype(F32)
    for r in range(8):
        qf[2 * r:2 * r + 2, :] = qs[:, r * 256:(r + 1) * 256]
    qsend[...] = qf[...].astype(BF16)
    qbuf[su] = qsend[...]

    pl.semaphore_wait(barrier, 6 + 7)

    def d_q1(k):
        return remote(qsend, qbuf.at[su], q1s.at[k], q1r.at[k], sub_peer(k))

    def d_c1(k):
        return remote(code, cbuf.at[su], c1s.at[k], c1r.at[k], sub_peer(k))

    loop(NSU, lambda k: d_q1(k).start())

    candp[...] = jnp.full((2, 256), -1, I32)
    candp[:, :CANDS] = cand_hbm[...]
    upper = jnp.where(iota((256, 256), 0) <= iota((256, 256), 1), 1.0, 0.0).astype(BF16)
    onehots, ranks = [], []
    before = jnp.zeros((128, 1), F32)
    for t in range(2):
        ids = candp[t:t + 1, :]
        dev = ids // D
        place = jnp.where(ids >= 0, (dev % NSU) * NSH + dev // NSU, -1)
        local = ids - dev * D + 1
        oh = jnp.where(iota((128, 256), 0) == place, 1.0, 0.0)
        ohb = oh.astype(BF16)
        cum = jnp.dot(ohb, upper, preferred_element_type=F32) + before
        rank = jnp.sum(oh * cum, axis=0, keepdims=True) - 1.0
        before = cum[:, 255:256]
        at = iota((CAP, 256), 0).astype(F32) == rank
        high = jnp.where(at, (local // 64).astype(F32), 0.0)
        low = jnp.where(at, (local % 64).astype(F32), 0.0)
        parts = dot_nt(jnp.concatenate([high, low], axis=0).astype(BF16), ohb)
        code[t * 8:t * 8 + 8, :] = parts[:8] * 64.0 + parts[8:]
        onehots.append(ohb)
        ranks.append(rank)

    cbuf[su] = code[...]
    loop(NSU, lambda k: d_c1(k).start())
    loop(NSU, lambda k: d_q1(k).wait())
    for i in range(NSU):
        block = qbuf[i].astype(F32)
        for r in range(8):
            for t in range(2):
                row = (i % 2) * 8 + t * 4 + i // 2
                q16f[row:row + 1, r * 256:(r + 1) * 256] = block[2 * r + t:2 * r + t + 1, :]
    for h in range(4):
        q16[h] = q16f[:, h * QW:(h + 1) * QW].astype(BF16)
    for c in range(2):
        qall[core * 2 + c, pl.ds(pl.multiple_of(sh * 16, 16), 16), :] = q16[core * 2 + c]

    def q_block(j):
        return qall.at[pl.ds(core * 2, 2), pl.ds(pl.multiple_of((sh ^ (j * step1)) * 16, 16), 16)]

    def d_q2(k):
        return remote(q_block(0), q_block(0), q2s.at[k], q2r.at[k], shard_peer(k * step1))

    def d_q3(j, k):
        return remote(q_block(j), q_block(j), q3s.at[j, k], q3r.at[j, k], shard_peer(k * step2))

    def d_c2(k):
        return remote(ctile.at[sh ^ k], crecv.at[sh], c2s.at[k], c2r.at[k], shard_peer(k))

    loop(4, lambda k: d_q2(k).start())
    loop(4, lambda k: d_q3(0, k).start())
    loop(NSU, lambda k: d_c1(k).wait())
    lane = iota((8, 128), 1)
    base = (sh % 8) * 16
    tiles = [jnp.zeros((8, 128), F32) for _ in range(NSH)]
    for i in range(NSU):
        for t in range(2):
            mine = pltpu.roll(cbuf[i, t * 8:t * 8 + 8, :], (NSU - su) * NSH, 1)
            here = lane == base + ((i % 2) * 8 + t * 4 + i // 2)
            for j in range(NSH):
                tiles[j] = jnp.where(here, jnp.broadcast_to(mine[:, j:j + 1], (8, 128)), tiles[j])
    for j in range(NSH):
        ctile[j] = tiles[j]
    crecv[sh] = ctile[sh]

    for j in range(1, 4):
        d_q2(j).wait()
        loop(4, lambda k: d_q3(j, k).start())

    loop(NSH, lambda k: d_c2(k).start())
    for j in range(4):
        loop(4, lambda k: d_q3(j, k).wait())
    def d_sib(c):
        part = qall.at[core * 2 + c]
        return remote(part, part, sibs.at[c], sibr.at[c], sub_peer(1))

    d_sib(0).start()
    d_sib(1).start()
    load_p.wait()

    def score(h, rows):
        cols = pl.ds(pl.multiple_of(h * QW, QW), QW)
        return dot_nt(p_v[rows, cols], qall[h])

    def score_half(i, c):
        rows = pl.ds(pl.multiple_of(i * 1024, 1024), 1024)
        st[rows, :] = score(core * 2, rows) + score(core * 2 + 1, rows)
        return c

    def score_third(i, c):
        rows = pl.ds(pl.multiple_of(i * 1024, 1024), 1024)
        st[rows, :] = st[rows, :] + score((1 - core) * 2, rows)
        return c

    lax.fori_loop(0, D // 1024, score_half, 0)
    loop(NSH, lambda k: d_c2(k).wait())
    first, second_ = crecv[0], crecv[8]
    for i in range(1, 8):
        first = first + crecv[i]
        second_ = second_ + crecv[8 + i]
    codes = jnp.concatenate([first, second_], axis=1).astype(I32) - 1
    valid = codes >= 0
    rows_of = [jnp.broadcast_to(codes[s:s + 1, :], (8, 256)) for s in range(CAP)]
    sub_iota = iota((8, 256), 0)
    d_sib(0).wait()
    lax.fori_loop(0, D // 1024, score_third, 0)
    d_sib(1).wait()

    def score_last(i, accs):
        base_row = pl.multiple_of(i * LAST, LAST)
        rows = pl.ds(base_row, LAST)
        vals = st[rows, :] + score((1 - core) * 2 + 1, rows)
        st[rows, :] = vals
        for j in range(LAST // 8):
            at = sub_iota + (base_row + j * 8)
            part = vals[j * 8:j * 8 + 8, :]
            accs = tuple(jnp.where(at == rows_of[s], part, a) for s, a in enumerate(accs))
        return accs

    accs = lax.fori_loop(0, D // LAST, score_last, tuple(jnp.zeros((8, 256), F32) for _ in range(CAP)))
    scores = jnp.concatenate([jnp.sum(a, axis=0, keepdims=True) for a in accs], axis=0) * (D ** -0.5)
    masked = jnp.where(valid, scores, NEG)
    m0 = jnp.max(masked, axis=0, keepdims=True)
    l0 = jnp.sum(jnp.where(valid, jnp.exp(masked - m0), 0.0), axis=0, keepdims=True)
    def fold(v):
        return jnp.concatenate([v[:, 0:128], v[:, 128:256]], axis=0)

    def unfold(v):
        return jnp.concatenate([v[0:1, :], v[1:2, :]], axis=1)

    stat1[0:2, :] = fold(m0)
    stat1[2:4, :] = fold(l0)
    stat1[4:8, :] = jnp.zeros((4, 128), F32)
    stat1r[su] = stat1[...]

    def d_s1(k):
        return remote(stat1, stat1r.at[su], s1s.at[k], s1r.at[k], sub_peer(k))

    loop(NSU, lambda k: d_s1(k).start())

    qp = qall[0, :, 0:128]
    qp = jnp.where(iota((NQ, 128), 1) < PREFIX, qp.astype(F32), 0.0).astype(BF16)

    def prefix(i, top):
        rows = pl.ds(pl.multiple_of(i * 512, 512), 512)
        part = dot_nt(p_v[rows, 0:128], qp) * (PREFIX ** -0.5)
        cst[rows, :] = part
        return jnp.maximum(top, jnp.max(part.reshape(64, 8, 256), axis=0))

    top = lax.fori_loop(0, D // 512, prefix, jnp.full((8, 256), NEG, F32))
    cm = jnp.max(top, axis=0, keepdims=True)

    def expsum(i, tot):
        rows = pl.ds(pl.multiple_of(i * 64, 64), 64)
        return tot + jnp.sum(jnp.exp(cst[rows, :] - cm).reshape(8, 8, 256), axis=0)

    tot = lax.fori_loop(0, D // 64, expsum, jnp.zeros((8, 256), F32))
    cl = jnp.sum(tot, axis=0, keepdims=True)

    loop(NSU, lambda k: d_s1(k).wait())

    def join(buf, n, row):
        top = buf[0, row:row + 2, :]
        for i in range(1, n):
            top = jnp.maximum(top, buf[i, row:row + 2, :])
        total = jnp.zeros((2, 128), F32)
        for i in range(n):
            total = total + buf[i, row + 2:row + 4, :] * jnp.exp(buf[i, row:row + 2, :] - top)
        return top, total

    m1, l1 = join(stat1r, NSU, 0)
    stat2[0:2, :] = m1
    stat2[2:4, :] = l1
    stat2[4:6, :] = fold(cm)
    stat2[6:8, :] = fold(cl)
    stat2r[sh] = stat2[...]

    def d_s2(k):
        return remote(stat2, stat2r.at[sh], s2s.at[k], s2r.at[k], shard_peer(k))

    loop(NSH, lambda k: d_s2(k).start())

    colt[:, 0:8] = codes.astype(F32).T
    colt[:, 8:16] = jnp.broadcast_to(m0, (8, 256)).T
    times = jnp.zeros((CAP, 256), F32)
    for s in range(CAP):
        times = times + jnp.where(codes == rows_of[s], 1.0, 0.0)
    colt[:, 16:24] = times.T

    def flip(i, c):
        rows = pl.ds(pl.multiple_of(i * 256, 256), 256)
        grown[:, rows] = st[rows, :].T
        return c

    lax.fori_loop(0, D // 256, flip, 0)

    def tally(i, c):
        rows = pl.ds(pl.multiple_of(i * 16, 16), 16)
        ct = colt[rows, 0:8].astype(I32)
        top = colt[rows, 8:9]
        ti = colt[rows, 16:24]
        for g in range(4):
            cols = iota((16, 512), 1) + g * 512
            here = slice(g * 512, (g + 1) * 512)
            val = jnp.zeros((16, 512), F32)
            for s in range(CAP):
                val = jnp.where(cols == ct[:, s:s + 1], ti[:, s:s + 1], val)
            count[rows, here] = val
            grown[rows, here] = jnp.where(val > 0.0, jnp.exp(grown[rows, here] * (D ** -0.5) - top), 0.0)
        return c

    lax.fori_loop(0, NQ // 16, tally, 0)
    loop(NSH, lambda k: d_s2(k).wait())
    m2, l2 = (unfold(v) for v in join(stat2r, NSH, 0))
    cm2, cl2 = join(stat2r, NSH, 4)

    scale = jnp.exp(m0 - m2) / l2
    probs = jnp.where(valid, jnp.exp(masked - m0), 0.0) * scale
    psend[0] = probs[:, 0:128]
    psend[1] = probs[:, 128:256]
    prtile[sh] = psend[sh // 8]

    def d_ps(k):
        return remote(psend.at[(sh ^ k) // 8], prtile.at[sh], ps_s.at[k], ps_r.at[k], shard_peer(k))

    loop(NSH, lambda k: d_ps(k).start())

    colt[:, 16:24] = jnp.broadcast_to(scale, (8, 256)).T

    def spread(i, c):
        rows = pl.ds(pl.multiple_of(i * 16, 16), 16)
        lows = pl.ds(pl.multiple_of(NQ + i * 16, 16), 16)
        f = colt[rows, 16:17]
        val = (grown[rows, :] * f).astype(BF16).astype(F32) * count[rows, :]
        hi = val.astype(BF16)
        whl[rows, :] = hi
        whl[lows, :] = (val - hi.astype(F32)).astype(BF16)
        return c

    lax.fori_loop(0, NQ // 16, spread, 0)

    def d_a(j):
        return remote(pool.at[j, 1 - core], ra.at[j], as_.at[j], ar_.at[j], sub_peer(1))

    def d_b(j, k):
        return remote(pool.at[j, core, pl.ds((a1 ^ k) * 4, 4)], rb.at[j, pl.ds(k * 4, 4)],
                      bs_.at[j, k], br_.at[j, k], shard_peer(k * step1))

    def d_e(j, k):
        return remote(rb.at[j, a2 ^ k], re.at[j, k], es_.at[j, k], er_.at[j, k], shard_peer(k * step2))

    def multiply(j):
        cols = slice(j * CW, (j + 1) * CW)
        part = jnp.dot(whl[...], p_v[:, cols], preferred_element_type=F32)
        part = part[:NQ] + part[NQ:]
        for i in range(NSH):
            for c in range(2):
                pool[j, c, i if c == 0 else (i % 4) * 4 + i // 4] = part[i * 16 + c * 8:i * 16 + c * 8 + 8, :]
        d_a(j).start()

    def forward(j):
        d_a(j).wait()
        for i in range(NSH):
            pool[j, core, i] = pool[j, core, i] + ra[j, i]
        loop(4, lambda k: d_b(j, k).start())

    def second(j):
        loop(4, lambda k: d_b(j, k).wait())
        for i in range(4):
            rb[j, i] = pool[j, core, a1 * 4 + i] + rb[j, 4 + i] + rb[j, 8 + i] + rb[j, 12 + i]
        loop(4, lambda k: d_e(j, k).start())

    def third(j):
        loop(4, lambda k: d_e(j, k).wait())
        tile = rb[j, a2] + re[j, 1] + re[j, 2] + re[j, 3]
        for t in range(2):
            for i in range(4):
                zsend[i, t * 8 + j:t * 8 + j + 1, :] = tile[t * 4 + i:t * 4 + i + 1, :]

    def at_once(j):
        loop(4, lambda k: d_b(j, k).wait())
        for i in range(4):
            tile = pool[j, core, a1 * 4 + i] + rb[j, 4 + i] + rb[j, 8 + i] + rb[j, 12 + i]
            for t in range(2):
                for e in range(4):
                    for g in range(CW // 128):
                        row = ((j - TWO_HOP) * 2 + t) * (CW // 128) + g
                        lsend[i * 4 + e, row:row + 1, :] = tile[t * 4 + e:t * 4 + e + 1, g * 128:(g + 1) * 128]

    def d_l(k):
        return remote(lsend.at[(a2 ^ (k // 4)) * 4 + (z ^ (k % 4))], lrecv.at[a2 * 4 + z], ls_.at[k], lr_.at[k],
                      (sh ^ ((k // 4) * step2), su ^ (2 * (k % 4))))

    multiply(0)
    multiply(1)
    forward(0)
    multiply(2)
    forward(1)
    multiply(3)
    forward(2)
    second(0)
    forward(3)
    second(1)

    loop(NSH, lambda k: d_ps(k).wait())
    outs = [[jnp.zeros((8, 128), F32) for _ in range(2)] for _ in range(NSU)]
    for h in range(NSH):
        mine = pltpu.roll(prtile[h], 128 - base, 1)
        here = lane == su * NSH + h
        for d in range(NSU):
            for t in range(2):
                col = (d % 2) * 8 + t * 4 + d // 2
                outs[d][t] = jnp.where(here, jnp.broadcast_to(mine[:, col:col + 1], (8, 128)), outs[d][t])
    coarse = jnp.concatenate([cm2, cl2, jnp.zeros((4, 128), F32)], axis=0)
    for d in range(NSU):
        for t in range(2):
            pusend[d, t * 8:t * 8 + 8, :] = outs[d][t]
        pusend[d, 16:24, :] = coarse
    purecv[su] = pusend[su]

    def d_pu(k):
        return remote(pusend.at[su ^ k], purecv.at[su], pu_s.at[k], pu_r.at[k], sub_peer(k))

    loop(NSU, lambda k: d_pu(k).start())

    third(0)
    third(1)
    for i in range(4):
        zsend[i, TWO_HOP:8, :] = jnp.zeros((8 - TWO_HOP, CW), F32)
        zsend[i, 8 + TWO_HOP:16, :] = jnp.zeros((8 - TWO_HOP, CW), F32)
    zr[z] = zsend[z]

    def d_z(k):
        return remote(zsend.at[z ^ k], zr.at[z], zs_.at[k], zr_.at[k], sub_peer(2 * k))

    loop(4, lambda k: d_z(k).start())
    at_once(2)
    at_once(3)
    lrecv[a2 * 4 + z] = lsend[a2 * 4 + z]
    loop(NSH, lambda k: d_l(k).start())

    loop(NSU, lambda k: d_pu(k).wait())
    for t in range(2):
        p = purecv[0, t * 8:t * 8 + 8, :]
        for i in range(1, NSU):
            p = p + purecv[i, t * 8:t * 8 + 8, :]
        p1 = p.astype(BF16)
        rest = p - p1.astype(F32)
        p2 = rest.astype(BF16)
        p3 = (rest - p2.astype(F32)).astype(BF16)
        y = jnp.dot(jnp.concatenate([p1.astype(F32), p2.astype(F32), p3.astype(F32)], axis=0).astype(BF16),
                    onehots[t], preferred_element_type=F32)
        y = y[0:8] + y[8:16] + y[16:24]
        row = jnp.sum(jnp.where(iota((CAP, 256), 0).astype(F32) == ranks[t], y, 0.0), axis=0, keepdims=True)
        probs_ref[t:t + 1, :] = row[:, :CANDS]
    top = purecv[0, 16:18, :]
    for i in range(1, NSU):
        top = jnp.maximum(top, purecv[i, 16:18, :])
    total = jnp.zeros((2, 128), F32)
    for i in range(NSU):
        total = total + purecv[i, 18:20, :] * jnp.exp(purecv[i, 16:18, :] - top)
    lse = top + jnp.log(total)
    spot = iota((2, 128), 0) * 128 + iota((2, 128), 1)
    for t in range(2):
        mine = jnp.where(spot == sh * 16 + core * 8 + t * 4 + z, lse, 0.0)
        lse_ref[0:1, t:t + 1] = jnp.sum(mine, keepdims=True)

    loop(4, lambda k: d_z(k).wait())
    final = zr[0] + zr[1] + zr[2] + zr[3]
    for t in range(2):
        for j in range(TWO_HOP):
            out_ref[t:t + 1, j * CW:(j + 1) * CW] = final[t * 8 + j:t * 8 + j + 1, :].astype(BF16)
    loop(NSH, lambda k: d_l(k).wait())
    final = lrecv[0]
    for i in range(1, NSH):
        final = final + lrecv[i]
    for j in range(TWO_HOP, CHUNKS):
        for t in range(2):
            for g in range(CW // 128):
                row = ((j - TWO_HOP) * 2 + t) * (CW // 128) + g
                out_ref[t:t + 1, j * CW + g * 128:j * CW + (g + 1) * 128] = final[row:row + 1, :].astype(BF16)


def shards(queries, passages, candidates):
    vmem = pl.BlockSpec(memory_space=pltpu.VMEM)
    V, DMA = pltpu.VMEM, pltpu.SemaphoreType.DMA
    lse, probs, pooled = pl.pallas_call(
        kernel,
        name="retrieve",
        out_shape=(
            jax.ShapeDtypeStruct((1, 2), F32),
            jax.ShapeDtypeStruct((2, CANDS), F32),
            jax.ShapeDtypeStruct((2, D), BF16),
        ),
        in_specs=[vmem, vmem, pl.BlockSpec(memory_space=pl.ANY)],
        out_specs=(vmem, vmem, vmem),
        scratch_shapes=[
            V((D, D), BF16), V((2, CANDS), I32), V((2, D), BF16), V((2, 256), I32), V((16, 256), F32), V((16, 256), BF16), V((16, 128), F32),
            V((NSU, 16, 256), BF16), V((NSU, 16, 128), F32), V((16, D), F32), V((4, 16, QW), BF16),
            V((4, NQ, QW), BF16), V((NSH, 8, 128), F32), V((NSH, 8, 128), F32),
            V((D, NQ), F32), V((D, NQ), F32),
            V((8, 128), F32), V((NSU, 8, 128), F32), V((8, 128), F32), V((NSH, 8, 128), F32),
            V((NQ, 128), F32), V((NQ, D), F32), V((NQ, D), F32), V((2 * NQ, D), BF16),
            V((CHUNKS, 2, NSH, 8, CW), F32), V((CHUNKS, NSH, 8, CW), F32), V((CHUNKS, NSH, 8, CW), F32),
            V((CHUNKS, 4, 8, CW), F32),
            V((4, 16, CW), F32), V((4, 16, CW), F32), V((NSH, 16, 128), F32), V((NSH, 16, 128), F32), V((2, 8, 128), F32), V((NSH, 8, 128), F32),
            V((NSU, 24, 128), F32), V((NSU, 24, 128), F32),
            DMA(()), DMA((2,)),
            DMA((NSU,)), DMA((NSU,)), DMA((NSU,)), DMA((NSU,)),
            DMA((4,)), DMA((4,)), DMA((4, 4)), DMA((4, 4)), DMA((NSH,)), DMA((NSH,)), DMA((2,)), DMA((2,)),
            DMA((NSU,)), DMA((NSU,)), DMA((NSH,)), DMA((NSH,)),
            DMA((NSH,)), DMA((NSH,)), DMA((NSU,)), DMA((NSU,)),
            DMA((CHUNKS,)), DMA((CHUNKS,)), DMA((CHUNKS, 4)), DMA((CHUNKS, 4)), DMA((CHUNKS, 4)), DMA((CHUNKS, 4)),
            DMA((4,)), DMA((4,)), DMA((NSH,)), DMA((NSH,)),
        ],
        compiler_params=pltpu.CompilerParams(
            collective_id=0, has_side_effects=True, vmem_limit_bytes=50 * 1024 * 1024
        ),
    )(candidates, queries, passages)
    return lse.reshape(2), probs, pooled


def solution(mesh):
    spec = P(("shard", "sub"), None)
    return jax.shard_map(shards, mesh=mesh, in_specs=(spec, spec, spec),
                         out_specs=(P(("shard", "sub")), spec, spec), check_vma=False)
```

```python
import jax
import jax.numpy as jnp
from jax import lax
from jax.experimental import pallas as pl
from jax.experimental.pallas import tpu as pltpu
from jax.sharding import PartitionSpec as P

NSH, NSU = 16, 8
NDEV = NSH * NSU
D = 2048
QW = D // 4
LAST = 1024
PREFIX = 64
CANDS = 200
CAP = 8
NQ = 256
CHUNKS = 4
CW = D // CHUNKS
TWO_HOP = CHUNKS - 2
NEG = -3.0e38
MESH = pl.DeviceIdType.MESH
F32, BF16, I32 = jnp.float32, jnp.bfloat16, jnp.int32


def iota(shape, dim):
    return lax.broadcasted_iota(I32, shape, dim)


def dot_nt(a, b):
    return lax.dot_general(a, b, (((1,), (1,)), ((), ())), preferred_element_type=F32)


def kernel(cand_hbm, q_hbm, p_hbm, lse_ref, probs_ref, out_ref,
           p_v, cand_v, q_v, candp, qf, qsend, code, qbuf, cbuf, q16f, q16, qall, ctile, crecv,
           st, cst, stat1, stat1r, stat2, stat2r, colt, count, grown, whl,
           pool, ra, rb, re, zsend, zr, lsend, lrecv, psend, prtile, pusend, purecv,
           p_sem, in_sem, q1s, q1r, c1s, c1r, q2s, q2r, q3s, q3r, c2s, c2r, sibs, sibr,
           s1s, s1r, s2s, s2r, ps_s, ps_r, pu_s, pu_r, as_, ar_, bs_, br_, es_, er_, zs_, zr_, ls_, lr_):
    sh, su = lax.axis_index("shard"), lax.axis_index("sub")
    core, z = su % 2, su // 2
    y, x = sh // 4, sh % 4
    a1, a2 = y + core * (x - y), x + core * (y - x)
    step1, step2 = 4 - 3 * core, 1 + 3 * core

    def sub_peer(k):
        return (sh, su ^ k)

    def shard_peer(k):
        return (sh ^ k, su)

    barrier = pltpu.get_barrier_semaphore()

    def greet(k, c):
        pl.semaphore_signal(barrier, inc=1, device_id=shard_peer(k), device_id_type=MESH)
        return c

    def greet_sub(k, c):
        pl.semaphore_signal(barrier, inc=1, device_id=sub_peer(k), device_id_type=MESH)
        return c

    for k in (8, 2, 4, 12, 1, 3):
        greet(k, 0)
    for k in (4, 5, 2, 3, 6, 7, 1):
        greet_sub(k, 0)
    load_p = pltpu.make_async_copy(p_hbm, p_v, p_sem)
    load_p.start()

    def loop(n, fn):
        for k in range(1, n):
            fn(k)

    def remote(src, dst, s, r, peer):
        return pltpu.make_async_remote_copy(src_ref=src, dst_ref=dst, send_sem=s, recv_sem=r,
                                            device_id=peer, device_id_type=MESH)

    qs = q_hbm[...].astype(F32)
    for r in range(8):
        qf[2 * r:2 * r + 2, :] = qs[:, r * 256:(r + 1) * 256]
    qsend[...] = qf[...].astype(BF16)
    qbuf[su] = qsend[...]

    pl.semaphore_wait(barrier, 6 + 7)

    def d_q1(k):
        return remote(qsend, qbuf.at[su], q1s.at[k], q1r.at[k], sub_peer(k))

    def d_c1(k):
        return remote(code, cbuf.at[su], c1s.at[k], c1r.at[k], sub_peer(k))

    loop(NSU, lambda k: d_q1(k).start())

    candp[...] = jnp.full((2, 256), -1, I32)
    candp[:, :CANDS] = cand_hbm[...]
    upper = jnp.where(iota((256, 256), 0) <= iota((256, 256), 1), 1.0, 0.0).astype(BF16)
    onehots, ranks = [], []
    before = jnp.zeros((128, 1), F32)
    for t in range(2):
        ids = candp[t:t + 1, :]
        dev = ids // D
        place = jnp.where(ids >= 0, (dev % NSU) * NSH + dev // NSU, -1)
        local = ids - dev * D + 1
        oh = jnp.where(iota((128, 256), 0) == place, 1.0, 0.0)
        ohb = oh.astype(BF16)
        cum = jnp.dot(ohb, upper, preferred_element_type=F32) + before
        rank = jnp.sum(oh * cum, axis=0, keepdims=True) - 1.0
        before = cum[:, 255:256]
        at = iota((CAP, 256), 0).astype(F32) == rank
        high = jnp.where(at, (local // 64).astype(F32), 0.0)
        low = jnp.where(at, (local % 64).astype(F32), 0.0)
        parts = dot_nt(jnp.concatenate([high, low], axis=0).astype(BF16), ohb)
        code[t * 8:t * 8 + 8, :] = parts[:8] * 64.0 + parts[8:]
        onehots.append(ohb)
        ranks.append(rank)

    cbuf[su] = code[...]
    loop(NSU, lambda k: d_c1(k).start())
    loop(NSU, lambda k: d_q1(k).wait())
    for i in range(NSU):
        block = qbuf[i].astype(F32)
        for r in range(8):
            for t in range(2):
                row = (i % 2) * 8 + t * 4 + i // 2
                q16f[row:row + 1, r * 256:(r + 1) * 256] = block[2 * r + t:2 * r + t + 1, :]
    for h in range(4):
        q16[h] = q16f[:, h * QW:(h + 1) * QW].astype(BF16)
    for c in range(2):
        qall[core * 2 + c, pl.ds(pl.multiple_of(sh * 16, 16), 16), :] = q16[core * 2 + c]

    def q_block(j):
        return qall.at[pl.ds(core * 2, 2), pl.ds(pl.multiple_of((sh ^ (j * step1)) * 16, 16), 16)]

    def d_q2(k):
        return remote(q_block(0), q_block(0), q2s.at[k], q2r.at[k], shard_peer(k * step1))

    def d_q3(j, k):
        return remote(q_block(j), q_block(j), q3s.at[j, k], q3r.at[j, k], shard_peer(k * step2))

    def d_c2(k):
        return remote(ctile.at[sh ^ k], crecv.at[sh], c2s.at[k], c2r.at[k], shard_peer(k))

    loop(4, lambda k: d_q2(k).start())
    loop(4, lambda k: d_q3(0, k).start())
    loop(NSU, lambda k: d_c1(k).wait())
    lane = iota((8, 128), 1)
    base = (sh % 8) * 16
    tiles = [jnp.zeros((8, 128), F32) for _ in range(NSH)]
    for i in range(NSU):
        for t in range(2):
            mine = pltpu.roll(cbuf[i, t * 8:t * 8 + 8, :], (NSU - su) * NSH, 1)
            here = lane == base + ((i % 2) * 8 + t * 4 + i // 2)
            for j in range(NSH):
                tiles[j] = jnp.where(here, jnp.broadcast_to(mine[:, j:j + 1], (8, 128)), tiles[j])
    for j in range(NSH):
        ctile[j] = tiles[j]
    crecv[sh] = ctile[sh]

    for j in range(1, 4):
        d_q2(j).wait()
        loop(4, lambda k: d_q3(j, k).start())

    loop(NSH, lambda k: d_c2(k).start())
    for j in range(4):
        loop(4, lambda k: d_q3(j, k).wait())
    def d_sib(c):
        part = qall.at[core * 2 + c]
        return remote(part, part, sibs.at[c], sibr.at[c], sub_peer(1))

    d_sib(0).start()
    d_sib(1).start()
    load_p.wait()

    def score(h, rows):
        cols = pl.ds(pl.multiple_of(h * QW, QW), QW)
        return dot_nt(p_v[rows, cols], qall[h])

    def score_half(i, c):
        rows = pl.ds(pl.multiple_of(i * 1024, 1024), 1024)
        st[rows, :] = score(core * 2, rows) + score(core * 2 + 1, rows)
        return c

    def score_third(i, c):
        rows = pl.ds(pl.multiple_of(i * 1024, 1024), 1024)
        st[rows, :] = st[rows, :] + score((1 - core) * 2, rows)
        return c

    lax.fori_loop(0, D // 1024, score_half, 0)
    loop(NSH, lambda k: d_c2(k).wait())
    first, second_ = crecv[0], crecv[8]
    for i in range(1, 8):
        first = first + crecv[i]
        second_ = second_ + crecv[8 + i]
    codes = jnp.concatenate([first, second_], axis=1).astype(I32) - 1
    valid = codes >= 0
    rows_of = [jnp.broadcast_to(codes[s:s + 1, :], (8, 256)) for s in range(CAP)]
    sub_iota = iota((8, 256), 0)
    d_sib(0).wait()
    lax.fori_loop(0, D // 1024, score_third, 0)
    d_sib(1).wait()

    def score_last(i, accs):
        base_row = pl.multiple_of(i * LAST, LAST)
        rows = pl.ds(base_row, LAST)
        vals = st[rows, :] + score((1 - core) * 2 + 1, rows)
        st[rows, :] = vals
        for j in range(LAST // 8):
            at = sub_iota + (base_row + j * 8)
            part = vals[j * 8:j * 8 + 8, :]
            accs = tuple(jnp.where(at == rows_of[s], part, a) for s, a in enumerate(accs))
        return accs

    accs = lax.fori_loop(0, D // LAST, score_last, tuple(jnp.zeros((8, 256), F32) for _ in range(CAP)))
    scores = jnp.concatenate([jnp.sum(a, axis=0, keepdims=True) for a in accs], axis=0) * (D ** -0.5)
    masked = jnp.where(valid, scores, NEG)
    m0 = jnp.max(masked, axis=0, keepdims=True)
    l0 = jnp.sum(jnp.where(valid, jnp.exp(masked - m0), 0.0), axis=0, keepdims=True)
    def fold(v):
        return jnp.concatenate([v[:, 0:128], v[:, 128:256]], axis=0)

    def unfold(v):
        return jnp.concatenate([v[0:1, :], v[1:2, :]], axis=1)

    stat1[0:2, :] = fold(m0)
    stat1[2:4, :] = fold(l0)
    stat1[4:8, :] = jnp.zeros((4, 128), F32)
    stat1r[su] = stat1[...]

    def d_s1(k):
        return remote(stat1, stat1r.at[su], s1s.at[k], s1r.at[k], sub_peer(k))

    loop(NSU, lambda k: d_s1(k).start())

    qp = qall[0, :, 0:128]
    qp = jnp.where(iota((NQ, 128), 1) < PREFIX, qp.astype(F32), 0.0).astype(BF16)

    def prefix(i, top):
        rows = pl.ds(pl.multiple_of(i * 512, 512), 512)
        part = dot_nt(p_v[rows, 0:128], qp) * (PREFIX ** -0.5)
        cst[rows, :] = part
        return jnp.maximum(top, jnp.max(part.reshape(64, 8, 256), axis=0))

    top = lax.fori_loop(0, D // 512, prefix, jnp.full((8, 256), NEG, F32))
    cm = jnp.max(top, axis=0, keepdims=True)

    def expsum(i, tot):
        rows = pl.ds(pl.multiple_of(i * 64, 64), 64)
        return tot + jnp.sum(jnp.exp(cst[rows, :] - cm).reshape(8, 8, 256), axis=0)

    tot = lax.fori_loop(0, D // 64, expsum, jnp.zeros((8, 256), F32))
    cl = jnp.sum(tot, axis=0, keepdims=True)

    loop(NSU, lambda k: d_s1(k).wait())

    def join(buf, n, row):
        top = buf[0, row:row + 2, :]
        for i in range(1, n):
            top = jnp.maximum(top, buf[i, row:row + 2, :])
        total = jnp.zeros((2, 128), F32)
        for i in range(n):
            total = total + buf[i, row + 2:row + 4, :] * jnp.exp(buf[i, row:row + 2, :] - top)
        return top, total

    m1, l1 = join(stat1r, NSU, 0)
    stat2[0:2, :] = m1
    stat2[2:4, :] = l1
    stat2[4:6, :] = fold(cm)
    stat2[6:8, :] = fold(cl)
    stat2r[sh] = stat2[...]

    def d_s2(k):
        return remote(stat2, stat2r.at[sh], s2s.at[k], s2r.at[k], shard_peer(k))

    loop(NSH, lambda k: d_s2(k).start())

    colt[:, 0:8] = codes.astype(F32).T
    colt[:, 8:16] = jnp.broadcast_to(m0, (8, 256)).T
    times = jnp.zeros((CAP, 256), F32)
    for s in range(CAP):
        times = times + jnp.where(codes == rows_of[s], 1.0, 0.0)
    colt[:, 16:24] = times.T

    def flip(i, c):
        rows = pl.ds(pl.multiple_of(i * 256, 256), 256)
        grown[:, rows] = st[rows, :].T
        return c

    lax.fori_loop(0, D // 256, flip, 0)

    def tally(i, c):
        rows = pl.ds(pl.multiple_of(i * 16, 16), 16)
        ct = colt[rows, 0:8].astype(I32)
        top = colt[rows, 8:9]
        ti = colt[rows, 16:24]
        for g in range(4):
            cols = iota((16, 512), 1) + g * 512
            here = slice(g * 512, (g + 1) * 512)
            val = jnp.zeros((16, 512), F32)
            for s in range(CAP):
                val = jnp.where(cols == ct[:, s:s + 1], ti[:, s:s + 1], val)
            count[rows, here] = val
            grown[rows, here] = jnp.where(val > 0.0, jnp.exp(grown[rows, here] * (D ** -0.5) - top), 0.0)
        return c

    lax.fori_loop(0, NQ // 16, tally, 0)
    loop(NSH, lambda k: d_s2(k).wait())
    m2, l2 = (unfold(v) for v in join(stat2r, NSH, 0))
    cm2, cl2 = join(stat2r, NSH, 4)

    scale = jnp.exp(m0 - m2) / l2
    probs = jnp.where(valid, jnp.exp(masked - m0), 0.0) * scale
    psend[0] = probs[:, 0:128]
    psend[1] = probs[:, 128:256]
    prtile[sh] = psend[sh // 8]

    def d_ps(k):
        return remote(psend.at[(sh ^ k) // 8], prtile.at[sh], ps_s.at[k], ps_r.at[k], shard_peer(k))

    loop(NSH, lambda k: d_ps(k).start())

    colt[:, 16:24] = jnp.broadcast_to(scale, (8, 256)).T

    def spread(i, c):
        rows = pl.ds(pl.multiple_of(i * 16, 16), 16)
        lows = pl.ds(pl.multiple_of(NQ + i * 16, 16), 16)
        f = colt[rows, 16:17]
        val = (grown[rows, :] * f).astype(BF16).astype(F32) * count[rows, :]
        hi = val.astype(BF16)
        whl[rows, :] = hi
        whl[lows, :] = (val - hi.astype(F32)).astype(BF16)
        return c

    lax.fori_loop(0, NQ // 16, spread, 0)

    def d_a(j):
        return remote(pool.at[j, 1 - core], ra.at[j], as_.at[j], ar_.at[j], sub_peer(1))

    def d_b(j, k):
        return remote(pool.at[j, core, pl.ds((a1 ^ k) * 4, 4)], rb.at[j, pl.ds(k * 4, 4)],
                      bs_.at[j, k], br_.at[j, k], shard_peer(k * step1))

    def d_e(j, k):
        return remote(rb.at[j, a2 ^ k], re.at[j, k], es_.at[j, k], er_.at[j, k], shard_peer(k * step2))

    def multiply(j):
        cols = slice(j * CW, (j + 1) * CW)
        part = jnp.dot(whl[...], p_v[:, cols], preferred_element_type=F32)
        part = part[:NQ] + part[NQ:]
        for i in range(NSH):
            for c in range(2):
                pool[j, c, i if c == 0 else (i % 4) * 4 + i // 4] = part[i * 16 + c * 8:i * 16 + c * 8 + 8, :]
        d_a(j).start()

    def forward(j):
        d_a(j).wait()
        for i in range(NSH):
            pool[j, core, i] = pool[j, core, i] + ra[j, i]
        loop(4, lambda k: d_b(j, k).start())

    def second(j):
        loop(4, lambda k: d_b(j, k).wait())
        for i in range(4):
            rb[j, i] = pool[j, core, a1 * 4 + i] + rb[j, 4 + i] + rb[j, 8 + i] + rb[j, 12 + i]
        loop(4, lambda k: d_e(j, k).start())

    def third(j):
        loop(4, lambda k: d_e(j, k).wait())
        tile = rb[j, a2] + re[j, 1] + re[j, 2] + re[j, 3]
        for t in range(2):
            for i in range(4):
                zsend[i, t * 8 + j:t * 8 + j + 1, :] = tile[t * 4 + i:t * 4 + i + 1, :]

    def at_once(j):
        loop(4, lambda k: d_b(j, k).wait())
        for i in range(4):
            tile = pool[j, core, a1 * 4 + i] + rb[j, 4 + i] + rb[j, 8 + i] + rb[j, 12 + i]
            for t in range(2):
                for e in range(4):
                    for g in range(CW // 128):
                        row = ((j - TWO_HOP) * 2 + t) * (CW // 128) + g
                        lsend[i * 4 + e, row:row + 1, :] = tile[t * 4 + e:t * 4 + e + 1, g * 128:(g + 1) * 128]

    def d_l(k):
        return remote(lsend.at[(a2 ^ (k // 4)) * 4 + (z ^ (k % 4))], lrecv.at[a2 * 4 + z], ls_.at[k], lr_.at[k],
                      (sh ^ ((k // 4) * step2), su ^ (2 * (k % 4))))

    multiply(0)
    multiply(1)
    forward(0)
    multiply(2)
    forward(1)
    multiply(3)
    forward(2)
    second(0)
    forward(3)
    second(1)

    loop(NSH, lambda k: d_ps(k).wait())
    outs = [[jnp.zeros((8, 128), F32) for _ in range(2)] for _ in range(NSU)]
    for h in range(NSH):
        mine = pltpu.roll(prtile[h], 128 - base, 1)
        here = lane == su * NSH + h
        for d in range(NSU):
            for t in range(2):
                col = (d % 2) * 8 + t * 4 + d // 2
                outs[d][t] = jnp.where(here, jnp.broadcast_to(mine[:, col:col + 1], (8, 128)), outs[d][t])
    coarse = jnp.concatenate([cm2, cl2, jnp.zeros((4, 128), F32)], axis=0)
    for d in range(NSU):
        for t in range(2):
            pusend[d, t * 8:t * 8 + 8, :] = outs[d][t]
        pusend[d, 16:24, :] = coarse
    purecv[su] = pusend[su]

    def d_pu(k):
        return remote(pusend.at[su ^ k], purecv.at[su], pu_s.at[k], pu_r.at[k], sub_peer(k))

    loop(NSU, lambda k: d_pu(k).start())

    third(0)
    third(1)
    for i in range(4):
        zsend[i, TWO_HOP:8, :] = jnp.zeros((8 - TWO_HOP, CW), F32)
        zsend[i, 8 + TWO_HOP:16, :] = jnp.zeros((8 - TWO_HOP, CW), F32)
    zr[z] = zsend[z]

    def d_z(k):
        return remote(zsend.at[z ^ k], zr.at[z], zs_.at[k], zr_.at[k], sub_peer(2 * k))

    loop(4, lambda k: d_z(k).start())
    at_once(2)
    at_once(3)
    lrecv[a2 * 4 + z] = lsend[a2 * 4 + z]
    loop(NSH, lambda k: d_l(k).start())

    loop(NSU, lambda k: d_pu(k).wait())
    for t in range(2):
        p = purecv[0, t * 8:t * 8 + 8, :]
        for i in range(1, NSU):
            p = p + purecv[i, t * 8:t * 8 + 8, :]
        p1 = p.astype(BF16)
        rest = p - p1.astype(F32)
        p2 = rest.astype(BF16)
        p3 = (rest - p2.astype(F32)).astype(BF16)
        y = jnp.dot(jnp.concatenate([p1.astype(F32), p2.astype(F32), p3.astype(F32)], axis=0).astype(BF16),
                    onehots[t], preferred_element_type=F32)
        y = y[0:8] + y[8:16] + y[16:24]
        row = jnp.sum(jnp.where(iota((CAP, 256), 0).astype(F32) == ranks[t], y, 0.0), axis=0, keepdims=True)
        probs_ref[t:t + 1, :] = row[:, :CANDS]
    top = purecv[0, 16:18, :]
    for i in range(1, NSU):
        top = jnp.maximum(top, purecv[i, 16:18, :])
    total = jnp.zeros((2, 128), F32)
    for i in range(NSU):
        total = total + purecv[i, 18:20, :] * jnp.exp(purecv[i, 16:18, :] - top)
    lse = top + jnp.log(total)
    spot = iota((2, 128), 0) * 128 + iota((2, 128), 1)
    for t in range(2):
        mine = jnp.where(spot == sh * 16 + core * 8 + t * 4 + z, lse, 0.0)
        lse_ref[0:1, t:t + 1] = jnp.sum(mine, keepdims=True)

    loop(4, lambda k: d_z(k).wait())
    final = zr[0] + zr[1] + zr[2] + zr[3]
    for t in range(2):
        for j in range(TWO_HOP):
            out_ref[t:t + 1, j * CW:(j + 1) * CW] = final[t * 8 + j:t * 8 + j + 1, :].astype(BF16)
    loop(NSH, lambda k: d_l(k).wait())
    final = lrecv[0]
    for i in range(1, NSH):
        final = final + lrecv[i]
    for j in range(TWO_HOP, CHUNKS):
        for t in range(2):
            for g in range(CW // 128):
                row = ((j - TWO_HOP) * 2 + t) * (CW // 128) + g
                out_ref[t:t + 1, j * CW + g * 128:j * CW + (g + 1) * 128] = final[row:row + 1, :].astype(BF16)


def shards(queries, passages, candidates):
    vmem = pl.BlockSpec(memory_space=pltpu.VMEM)
    V, DMA = pltpu.VMEM, pltpu.SemaphoreType.DMA
    lse, probs, pooled = pl.pallas_call(
        kernel,
        name="retrieve",
        out_shape=(
            jax.ShapeDtypeStruct((1, 2), F32),
            jax.ShapeDtypeStruct((2, CANDS), F32),
            jax.ShapeDtypeStruct((2, D), BF16),
        ),
        in_specs=[vmem, vmem, pl.BlockSpec(memory_space=pl.ANY)],
        out_specs=(vmem, vmem, vmem),
        scratch_shapes=[
            V((D, D), BF16), V((2, CANDS), I32), V((2, D), BF16), V((2, 256), I32), V((16, 256), F32), V((16, 256), BF16), V((16, 128), F32),
            V((NSU, 16, 256), BF16), V((NSU, 16, 128), F32), V((16, D), F32), V((4, 16, QW), BF16),
            V((4, NQ, QW), BF16), V((NSH, 8, 128), F32), V((NSH, 8, 128), F32),
            V((D, NQ), F32), V((D, NQ), F32),
            V((8, 128), F32), V((NSU, 8, 128), F32), V((8, 128), F32), V((NSH, 8, 128), F32),
            V((NQ, 128), F32), V((NQ, D), F32), V((NQ, D), F32), V((2 * NQ, D), BF16),
            V((CHUNKS, 2, NSH, 8, CW), F32), V((CHUNKS, NSH, 8, CW), F32), V((CHUNKS, NSH, 8, CW), F32),
            V((CHUNKS, 4, 8, CW), F32),
            V((4, 16, CW), F32), V((4, 16, CW), F32), V((NSH, 16, 128), F32), V((NSH, 16, 128), F32), V((2, 8, 128), F32), V((NSH, 8, 128), F32),
            V((NSU, 24, 128), F32), V((NSU, 24, 128), F32),
            DMA(()), DMA((2,)),
            DMA((NSU,)), DMA((NSU,)), DMA((NSU,)), DMA((NSU,)),
            DMA((4,)), DMA((4,)), DMA((4, 4)), DMA((4, 4)), DMA((NSH,)), DMA((NSH,)), DMA((2,)), DMA((2,)),
            DMA((NSU,)), DMA((NSU,)), DMA((NSH,)), DMA((NSH,)),
            DMA((NSH,)), DMA((NSH,)), DMA((NSU,)), DMA((NSU,)),
            DMA((CHUNKS,)), DMA((CHUNKS,)), DMA((CHUNKS, 4)), DMA((CHUNKS, 4)), DMA((CHUNKS, 4)), DMA((CHUNKS, 4)),
            DMA((4,)), DMA((4,)), DMA((NSH,)), DMA((NSH,)),
        ],
        compiler_params=pltpu.CompilerParams(
            collective_id=0, has_side_effects=True, vmem_limit_bytes=50 * 1024 * 1024
        ),
    )(candidates, queries, passages)
    return lse.reshape(2), probs, pooled


def solution(mesh):
    spec = P(("shard", "sub"), None)
    return jax.shard_map(shards, mesh=mesh, in_specs=(spec, spec, spec),
                         out_specs=(P(("shard", "sub")), spec, spec), check_vma=False)
```
